32 devices in a mesh: sta: 8 (over z, y), tpl: 4 (over x, core).
Axes of the slice: x: 2, y: 2, z: 4, core: 2. Of those that a mesh axis runs over, the one named last changes fastest.
Arguments:
- station_data: float32 [3, 128, 3200], P(None, ('sta', 'tpl'))
- channel_mask: int32 [3, 128], P(None, 'sta'), may hold values 0 or 1
- template_waves: bfloat16 [32, 8, 3, 640], P('tpl', 'sta')
- pick_station: int32 [32, 8], P('tpl'), may hold values from 0 to 127, as said below
- pick_lag: int32 [32, 8], P('tpl'), may hold values from 0 to 1024, as said below
Outputs:
- network_stack: float32 [1536, 32], P('sta', 'tpl')
The draws below stay inside these ranges and needn't reach their ends.
Inputs may be any that keep to these rules, and one draw needn't show every extreme that they name: `pick_station`: the 8 picks of a template lie on distinct stations. Within each aligned block of 8 templates and for each pick index p, at most 2 templates have pick p on one aligned block of 16 stations; for every p this is reached on some block of stations. `pick_lag`: every template has a pick at lag 0 and a pick at lag 1024.
All inputs are finite; a program needn't handle non-finite values. No bound on the sum of `channel_mask` on one device may be relied on, other than what follows from the above.
Results may differ from the reference program's by a relative error of at most 0.0041.
Values may be sent and summed in bfloat16 or wider, within the bound.
A program may use at most 64 MiB of HBM per device.

```python
import math
import jax
import jax.numpy as jnp
from jax import lax

S_DEV = 16
NT = 1536
L = 640
LAGS = 1024
BLOCK = 128
STATIONS = 128
PICKS = 8
TPL_GROUP = 8
TEMPLATES = 32
CAP = 2
SAMPLES = 3200
N_STA = 8
N_TPL = 4


def envelope(key, leading, length):
    blocks = length // 16 + 1
    levels = jnp.exp(jax.random.uniform(key, leading + (blocks,), minval=0.0, maxval=math.log(10.0)))
    return jnp.repeat(levels, 16, axis=-1)[..., :length]


def arrivals(key, shape):
    key_a, key_b, key_c = jax.random.split(key, 3)
    hits = jax.random.randint(key_a, (1,) + shape[1:], 0, 192) == 0
    sizes = jax.random.uniform(key_b, shape, minval=40.0, maxval=80.0)
    signs = jnp.where(jax.random.randint(key_c, shape, 0, 2) == 0, -1.0, 1.0)
    return jnp.where(hits, sizes * signs, 0.0)


def draw_station_data(key, part):
    key_a = jax.random.fold_in(key, 0)
    key_b = jax.random.fold_in(key, 1)
    key_c = jax.random.fold_in(key, 2)
    key_e = jax.random.fold_in(key, 4)
    shape = (3, STATIONS, SAMPLES)
    level = jnp.exp(jax.random.uniform(key_b, (3, STATIONS, 1), minval=0.0, maxval=math.log(10.0)))
    shaping = envelope(key_c, (1, STATIONS), SAMPLES)
    impulses = arrivals(key_e, shape)
    base = jnp.clip(jax.random.normal(key_a, shape), -6.0, 6.0)
    return (base + impulses) * shaping * level


def draw_template_waves(key, part):
    key_a, key_b, key_c = jax.random.split(key, 3)
    shape = (TEMPLATES, PICKS, 3, L)
    level = jnp.exp(jax.random.uniform(key_b, (TEMPLATES, PICKS, 3, 1), minval=0.0, maxval=math.log(10.0)))
    shaping = envelope(key_c, (TEMPLATES, PICKS, 1), L)
    base = jnp.clip(jax.random.normal(key_a, shape), -6.0, 6.0)
    return (base * shaping * level).astype(jnp.bfloat16)


def one_group(group_key):
    key_a, key_b, key_c = jax.random.split(group_key, 3)
    leader = jax.random.randint(key_a, (), 0, N_STA)
    order = jax.random.permutation(key_b, TPL_GROUP)
    rest = TPL_GROUP - 2 * CAP
    round_count = rest // (N_STA - 2) + 1
    round_keys = jax.random.split(key_c, round_count)
    shuffles = jax.vmap(lambda round_key: jax.random.permutation(round_key, N_STA - 2))(round_keys).reshape(-1)
    position = jnp.arange(TPL_GROUP)
    later = jnp.clip(position - 2 * CAP, 0, round_count * (N_STA - 2) - 1)
    offsets = jnp.where(position < CAP, 0, jnp.where(position < 2 * CAP, N_STA - 1, shuffles[later] + 1))
    by_position = (leader + offsets) % N_STA
    return by_position[order]


def draw_pick_station(key, part):
    key_a, key_b = jax.random.split(key, 2)
    group_keys = jax.vmap(lambda index: jax.random.fold_in(key_a, index))(jnp.arange(N_TPL))
    centres = jax.vmap(one_group)(group_keys).reshape(TEMPLATES, 1)
    shifts = jax.random.randint(key_b, (TEMPLATES, 1), 0, S_DEV)
    column = jnp.arange(PICKS).reshape(1, PICKS)
    owners = (centres + column) % N_STA
    locals_here = shifts % S_DEV
    return (owners * S_DEV + locals_here).astype(jnp.int32)


def draw_pick_lag(key, part):
    key_a, key_b, key_c = jax.random.split(key, 3)
    lags = jax.random.randint(key_a, (TEMPLATES, PICKS), 0, LAGS + 1)
    zero_at = jax.random.randint(key_b, (TEMPLATES, 1), 0, PICKS)
    top_at = (zero_at + jax.random.randint(key_c, (TEMPLATES, 1), 1, PICKS)) % PICKS
    column = jnp.arange(PICKS).reshape(1, PICKS)
    lags = jnp.where(column == zero_at, 0, lags)
    return jnp.where(column == top_at, LAGS, lags).astype(jnp.int32)


def with_ends(values, own_key, low, largest):
    longest = values.shape.index(max(values.shape))
    spots = []
    for shift in (0, 1):
        where = [jax.random.randint(jax.random.fold_in(own_key, axis), (), 0, length) for axis, length in enumerate(values.shape)]
        where[longest] = (where[longest] + shift) % values.shape[longest]
        spots.append(tuple(where))
    return values.at[spots[0]].set(low).at[spots[1]].set(largest)


def setup_inputs(seed: int = 0) -> dict:
    streams_of = jax.random.split(jax.random.key(seed), 6)
    station_data = draw_station_data(jax.random.fold_in(streams_of[5], 71), 0)
    channel_mask = with_ends((jax.random.randint(streams_of[1], (3, STATIONS), 0, 10) < 9).astype(jnp.int32), jax.random.fold_in(streams_of[1], 1), 0, 1)
    template_waves = draw_template_waves(jax.random.fold_in(streams_of[5], 71), 0)
    pick_station = draw_pick_station(jax.random.fold_in(streams_of[5], 71), 0)
    pick_lag = draw_pick_lag(jax.random.fold_in(streams_of[5], 71), 0)
    return dict(station_data=station_data, channel_mask=channel_mask, template_waves=template_waves, pick_station=pick_station, pick_lag=pick_lag)


epsilon = 1e-05

def window_scales(samples):
    leading = jnp.zeros(samples.shape[:-1] + (1,), jnp.float32)
    sum_one = jnp.concatenate([leading, jnp.cumsum(samples, axis=-1)], axis=-1)
    sum_two = jnp.concatenate([leading, jnp.cumsum(samples * samples, axis=-1)], axis=-1)
    starts = NT + LAGS
    mean_one = (sum_one[..., L:L + starts] - sum_one[..., :starts]) / L
    mean_two = (sum_two[..., L:L + starts] - sum_two[..., :starts]) / L
    return 1.0 / (L * jnp.sqrt(mean_two - mean_one * mean_one + epsilon))

def unit_waves(raw_waves):
    values = raw_waves.astype(jnp.float32)
    centred = values - lax.optimization_barrier(jnp.mean(values, axis=-1, keepdims=True))
    spread = jnp.sqrt(lax.optimization_barrier(jnp.mean(centred * centred, axis=-1, keepdims=True)) + epsilon)
    return (centred / spread).astype(jnp.bfloat16)

def toeplitz_rows(units):
    batch = units.shape[0]
    row_width = units.shape[1] + BLOCK
    padded = jnp.concatenate([units, jnp.zeros((batch, BLOCK), units.dtype)], axis=1)
    tiled = jnp.tile(padded, (1, BLOCK))
    trimmed = tiled[:, :BLOCK * (row_width - 1)].reshape(batch, BLOCK, row_width - 1)
    return jnp.concatenate([trimmed, jnp.zeros((batch, BLOCK, 1), units.dtype)], axis=2)

def frames_of(windows):
    batch, length = windows.shape
    row_total = (length - L) // BLOCK
    columns = [windows[:, BLOCK * offset:BLOCK * offset + row_total * BLOCK].reshape(batch, row_total, BLOCK) for offset in range((L + BLOCK) // BLOCK)]
    return jnp.concatenate(columns, axis=2)

def correlate(windows, units):
    frames = frames_of(windows).astype(jnp.float32)
    toeplitz = toeplitz_rows(units).astype(jnp.float32)
    product = jnp.einsum('bim,bjm->bij', frames, toeplitz, precision=lax.Precision.HIGHEST)
    return product.reshape(windows.shape[0], -1)

def reference(station_data, channel_mask, template_waves, pick_station, pick_lag):
    scales = window_scales(station_data)
    rounded = station_data.astype(jnp.bfloat16)
    weights = channel_mask.astype(jnp.float32).T

    def one_template(inputs):
        raw_waves, stations, pick_lags = inputs
        units = unit_waves(raw_waves)

        def take_window(station, lag_here):
            zero_start = jnp.zeros((), jnp.int32)
            station_start = station.astype(jnp.int32)
            lag_start = lag_here.astype(jnp.int32)
            window = lax.dynamic_slice(rounded, (zero_start, station_start, lag_start), (3, 1, NT + L))[:, 0]
            scale_rows = lax.dynamic_slice(scales, (zero_start, station_start, lag_start), (3, 1, NT))[:, 0]
            return (window, scale_rows)
        windows, factors = jax.vmap(take_window)(stations, pick_lags)
        correlation = correlate(windows.reshape(PICKS * 3, NT + L), units.reshape(PICKS * 3, L)).reshape(PICKS, 3, NT)
        available = weights[stations]
        return lax.optimization_barrier(jnp.sum(correlation * factors * available[:, :, None], axis=(0, 1)))
    network = lax.map(one_template, (template_waves, pick_station, pick_lag))
    return network.T
```

```python
import functools

import jax
import jax.numpy as jnp
from jax import lax
from jax.experimental import pallas as pl
from jax.experimental.pallas import tpu as pltpu
from jax.sharding import PartitionSpec as P

NT = 1536
L = 640
LAGS = 1024
W = 128
EPS = 1e-05
MESH = pl.DeviceIdType.MESH
F32 = jnp.float32
BF16 = jnp.bfloat16

NB = NT // W
MR = 16
WL = L // W
KB = WL + 2


def turn(values, amount):
    for bit in range(7):
        on = (jnp.full(values.shape, amount, jnp.int32) >> bit) & 1
        values = jnp.where(on == 1, pltpu.roll(values, 1 << bit, axis=1), values)
    return values


def kernel(
    dims,
    data_ref,
    waves_ref,
    mask_ref,
    ps_ref,
    pl_ref,
    out_ref,
    buf0,
    buf1,
    buf2,
    s1_ref,
    s2_ref,
    sc_ref,
    uw_ref,
    pkt_ref,
    pk_ref,
    acc_ref,
    part_ref,
    land_ref,
    base_tab,
    b_tab,
    st_tab,
    tp_tab,
    d_send,
    d_recv,
    p_send,
    p_recv,
    r_send,
    r_recv,
):
    S, N, SL, G, CAP, RPS, RG, ND, NBD = dims
    X = N // 2
    NS = S * CAP
    bufs = (buf0, buf1, buf2)
    me = lax.axis_index("sta")
    g = lax.axis_index("tpl")
    core = lax.rem(g, 2)
    xpos = g // 2
    mate = g + 1 - 2 * core
    peers = [{"sta": me, "tpl": mate}]
    far = []
    for k in range(1, X):
        far.append(lax.rem(xpos + k, X) * 2 + core)
        peers.append({"sta": me, "tpl": far[-1]})
    for k in range(1, S):
        peers.append({"sta": lax.rem(me + k, S), "tpl": g})

    barrier = pltpu.get_barrier_semaphore()
    for peer in peers:
        pl.semaphore_signal(barrier, inc=1, device_id=peer, device_id_type=MESH)

    own_row = pl.multiple_of(g * RG, 8)
    for c in range(3):
        bufs[c][pl.ds(N * RG, 16), :] = jnp.zeros((16, W), F32)
        bufs[c][pl.ds(own_row + RG - 8, 8), :] = jnp.zeros((8, W), F32)
        for b in range(RPS):
            bufs[c][pl.ds(own_row + b, SL, stride=RPS), :] = data_ref[c, :, b * W : (b + 1) * W]

    pl.semaphore_wait(barrier, len(peers))

    def record_copy(c, kind):
        if kind == 0:
            source, target = g, mate
        elif kind < X:
            source, target = g, far[kind - 1]
        else:
            source, target = lax.rem(xpos + X - (kind - X + 1), X) * 2 + core, mate
        rows = pl.ds(pl.multiple_of(source * RG, 8), RG)
        return pltpu.make_async_remote_copy(
            src_ref=bufs[c].at[rows],
            dst_ref=bufs[c].at[rows],
            send_sem=d_send.at[c, kind],
            recv_sem=d_recv.at[c, kind],
            device_id={"sta": me, "tpl": target},
            device_id_type=MESH,
        )

    for c in range(3):
        for kind in list(range(1, X)) + [0]:
            record_copy(c, kind).start()

    for c in range(3):
        values = waves_ref[0, c].astype(F32)
        centred = values - jnp.mean(values, axis=-1, keepdims=True)
        spread = jnp.sqrt(jnp.mean(centred * centred, axis=-1, keepdims=True) + EPS)
        unit = centred / spread
        for a in range(WL):
            uw_ref[:, 3 * a + c, :] = unit[:, a * W : (a + 1) * W]

    def packet_step(d, _):
        count = jnp.int32(0)
        chosen = [jnp.int32(0)] * CAP
        low = d * SL * N
        for t in range(G):
            station = ps_ref[t, me]
            mine = jnp.logical_and(station >= low, station < low + SL * N).astype(jnp.int32)
            for j in range(CAP):
                chosen[j] = jnp.where(mine * (count + 1) == j + 1, t, chosen[j])
            count = count + mine
        for j in range(CAP):
            row = pl.multiple_of((d * CAP + j) * 16, 16)
            pkt_ref[pl.ds(row, 16), :] = uw_ref[chosen[j]].astype(BF16)
        return 0

    lax.fori_loop(0, S, packet_step, 0)

    def packet_copy(k):
        target = lax.rem(me + k, S)
        return pltpu.make_async_remote_copy(
            src_ref=pkt_ref.at[pl.ds(pl.multiple_of(target * CAP * 16, 16), CAP * 16)],
            dst_ref=pk_ref.at[pl.ds(pl.multiple_of(me * CAP * 16, 16), CAP * 16)],
            send_sem=p_send.at[k - 1],
            recv_sem=p_recv.at[k - 1],
            device_id={"sta": target, "tpl": g},
            device_id_type=MESH,
        )

    for k in range(1, S):
        packet_copy(k).start()
    own_packet = pl.ds(pl.multiple_of(me * CAP * 16, 16), CAP * 16)
    pk_ref[own_packet, :] = pkt_ref[own_packet, :]

    def table_step(p, _):
        count = jnp.int32(0)
        stations = [jnp.int32(0)] * CAP
        lags = [jnp.int32(0)] * CAP
        low = me * SL * N
        for t in range(G):
            station = ps_ref[t, p]
            lag = pl_ref[t, p]
            mine = jnp.logical_and(station >= low, station < low + SL * N).astype(jnp.int32)
            tp_tab[t * S + p] = jnp.where(mine == 1, p * CAP + jnp.minimum(count, CAP - 1), NS)
            for j in range(CAP):
                here = mine * (count + 1) == j + 1
                stations[j] = jnp.where(here, station - low, stations[j])
                lags[j] = jnp.where(here, lag, lags[j])
            count = count + mine
        for j in range(CAP):
            holder = stations[j] // SL
            base_tab[p * CAP + j] = holder * RG + (stations[j] - holder * SL) * RPS + lags[j] // W
            b_tab[p * CAP + j] = lax.rem(lags[j], W)
            st_tab[p * CAP + j] = stations[j]
        return 0

    lax.fori_loop(0, S, table_step, 0)

    lane = lax.broadcasted_iota(jnp.int32, (8, W), 1)
    sub = lax.broadcasted_iota(jnp.int32, (8, W), 0)
    ones_k = lax.broadcasted_iota(jnp.int32, (2 * W, W), 0)
    ones_r = lax.broadcasted_iota(jnp.int32, (2 * W, W), 1)
    window = jnp.logical_and(ones_k >= ones_r, ones_k < ones_r + W).astype(F32).astype(BF16)

    def window_sum(values):
        high = values.astype(BF16)
        rest = values - high.astype(F32)
        middle = rest.astype(BF16)
        low = (rest - middle.astype(F32)).astype(BF16)
        total = jnp.dot(low, window, preferred_element_type=F32)
        total += jnp.dot(middle, window, preferred_element_type=F32)
        return total + jnp.dot(high, window, preferred_element_type=F32)

    tail = pl.ds(N * RG, 16)
    s1_ref[tail, :] = jnp.zeros((16, W), F32)
    s2_ref[tail, :] = jnp.zeros((16, W), F32)
    sc_ref[tail, :] = jnp.zeros((16, W), F32)
    acc_ref[NS] = jnp.zeros((MR, W), F32)

    def scales_of(buf):
        def sums(h, _):
            row = pl.multiple_of(h * RG, 8)
            x = jnp.concatenate([buf[pl.ds(row, RG), :], buf[pl.ds(row + 1, RG), :]], axis=1)
            s1_ref[pl.ds(row, RG), :] = window_sum(x)
            s2_ref[pl.ds(row, RG), :] = window_sum(x * x)
            return 0

        lax.fori_loop(0, N, sums, 0)

        def finish(h, _):
            row = pl.multiple_of(h * RG, 8)
            one = s1_ref[pl.ds(row, RG), :]
            two = s2_ref[pl.ds(row, RG), :]
            for a in range(1, WL):
                one += s1_ref[pl.ds(row + a, RG), :]
                two += s2_ref[pl.ds(row + a, RG), :]
            one = one * (1.0 / L)
            two = two * (1.0 / L)
            sc_ref[pl.ds(row, RG), :] = lax.rsqrt(two - one * one + EPS) * (1.0 / L)
            return 0

        lax.fori_loop(0, N, finish, 0)

    def slots_of(c, buf):
        def slot_step(slot, _):
            base = base_tab[slot]
            shift = b_tab[slot]
            weight = mask_ref[c, st_tab[slot]].astype(F32)
            rows = pl.ds(pl.multiple_of(slot * 16, 16), 16)
            unit = turn(pk_ref[rows, :].astype(F32), shift)
            row_lane = lane[0:1]
            zero_row = jnp.zeros((1, W), F32)
            spread = []
            for a in range(WL + 1):
                now = unit[3 * a + c : 3 * a + c + 1] if a < WL else zero_row
                before = unit[3 * (a - 1) + c : 3 * (a - 1) + c + 1] if a > 0 else zero_row
                spread.append(jnp.broadcast_to(jnp.where(row_lane < shift, before, now), (8, W)))
            zero_tile = jnp.zeros((8, W), F32)
            strips = []
            for j in range(W // 8):
                turned = [pltpu.roll(v, 8 * j, axis=1, stride=1, stride_axis=0) for v in spread]
                turned = [zero_tile] + turned + [zero_tile]
                keep = lane >= sub + 8 * j
                strips.append(
                    jnp.concatenate(
                        [jnp.where(keep, turned[a + 1], turned[a]) for a in range(KB)], axis=1
                    )
                )
            toeplitz = jnp.concatenate(strips, axis=0).astype(BF16)
            frames = jnp.concatenate(
                [buf[pl.ds(base + a, MR), :] for a in range(KB)], axis=1
            ).astype(BF16)
            corr = lax.dot_general(
                frames, toeplitz, (((1,), (1,)), ((), ())), preferred_element_type=F32
            )
            back = lax.rem(W - shift, W)
            first = turn(sc_ref[pl.ds(base, MR), :], back)
            second = turn(sc_ref[pl.ds(base + 1, MR), :], back)
            wide = lax.broadcasted_iota(jnp.int32, (MR, W), 1)
            term = corr * (jnp.where(wide < W - shift, first, second) * weight)
            if c == 0:
                acc_ref[slot] = term
            else:
                acc_ref[slot] += term
            return 0

        lax.fori_loop(0, NS, slot_step, 0, unroll=2)

    def pass_on(c):
        for kind in range(1, X):
            record_copy(c, kind).wait_recv()
            record_copy(c, X - 1 + kind).start()

    pass_on(0)
    for c in range(3):
        record_copy(c, 0).wait_recv()
        for kind in range(X, 2 * X - 1):
            record_copy(c, kind).wait_recv()
        scales_of(bufs[c])
        if c < 2:
            pass_on(c + 1)
        if c == 0:
            for k in range(1, S):
                packet_copy(k).wait_recv()
        slots_of(c, bufs[c])

    for t in range(G):

        def add_pick(p, total):
            return total + acc_ref[tp_tab[t * S + p]]

        total = lax.fori_loop(0, S, add_pick, jnp.zeros((MR, W), F32), unroll=8)
        part_ref[pl.ds(t, MR, stride=G), :] = total

    def part_rows(d):
        return pl.ds(pl.multiple_of((d * ND // W) * G, 8), NBD * G)

    def sum_copy(k):
        target = lax.rem(me + k, S)
        return pltpu.make_async_remote_copy(
            src_ref=part_ref.at[part_rows(target)],
            dst_ref=land_ref.at[pl.ds((k - 1) * NBD * G, NBD * G)],
            send_sem=r_send.at[k - 1],
            recv_sem=r_recv.at[k - 1],
            device_id={"sta": target, "tpl": g},
            device_id_type=MESH,
        )

    for k in range(1, S):
        sum_copy(k).start()
    total = part_ref[part_rows(me), :]
    for k in range(1, S):
        sum_copy(k).wait_recv()
        total = total + land_ref[pl.ds((k - 1) * NBD * G, NBD * G), :]
    offset = lax.rem(me * ND, W)
    turned = pltpu.roll(total, lax.rem(W - offset, W), axis=1)
    wide = lax.broadcasted_iota(jnp.int32, (G, W), 1)
    pieces = []
    for b in range(-(-ND // W)):
        now = turned[b * G : (b + 1) * G]
        after = turned[(b + 1) * G : (b + 2) * G] if b + 1 < NBD else now
        pieces.append(jnp.where(wide < W - offset, now, after))
    out_ref[...] = jnp.concatenate(pieces, axis=1)[:, :ND]

    for c in range(3):
        for kind in range(2 * X - 1):
            record_copy(c, kind).wait_send()
    for k in range(1, S):
        packet_copy(k).wait_send()
        sum_copy(k).wait_send()


def body(S, N, station_data, channel_mask, template_waves, pick_station, pick_lag):
    SL, samples = station_data.shape[1], station_data.shape[2]
    G, picks = pick_station.shape
    assert picks == S and template_waves.shape[1] == 1
    CAP = max(2, G // 8)
    RPS = samples // W
    RG = -(-(SL * RPS) // 8) * 8
    ND = NT // S
    NBD = max(-(-(d * ND % W + ND) // W) for d in range(S))
    X = N // 2
    NS = S * CAP
    dims = (S, N, SL, G, CAP, RPS, RG, ND, NBD)
    rows = N * RG + 16
    vmem = pl.BlockSpec(memory_space=pltpu.VMEM)
    smem = pl.BlockSpec(memory_space=pltpu.SMEM)
    flops = 2 * NS * 3 * MR * W * KB * W
    result = pl.pallas_call(
        functools.partial(kernel, dims),
        out_shape=jax.ShapeDtypeStruct((G, ND), F32),
        in_specs=[vmem, vmem, smem, smem, smem],
        out_specs=vmem,
        scratch_shapes=[
            pltpu.VMEM((rows, W), F32),
            pltpu.VMEM((rows, W), F32),
            pltpu.VMEM((rows, W), F32),
            pltpu.VMEM((rows, W), F32),
            pltpu.VMEM((rows, W), F32),
            pltpu.VMEM((rows, W), F32),
            pltpu.VMEM((G, 16, W), F32),
            pltpu.VMEM((NS * 16, W), BF16),
            pltpu.VMEM((NS * 16, W), BF16),
            pltpu.VMEM((NS + 1, MR, W), F32),
            pltpu.VMEM((MR * G, W), F32),
            pltpu.VMEM(((S - 1) * NBD * G, W), F32),
            pltpu.SMEM((NS,), jnp.int32),
            pltpu.SMEM((NS,), jnp.int32),
            pltpu.SMEM((NS,), jnp.int32),
            pltpu.SMEM((G * S,), jnp.int32),
            pltpu.SemaphoreType.DMA((3, 2 * X - 1)),
            pltpu.SemaphoreType.DMA((3, 2 * X - 1)),
            pltpu.SemaphoreType.DMA((S - 1,)),
            pltpu.SemaphoreType.DMA((S - 1,)),
            pltpu.SemaphoreType.DMA((S - 1,)),
            pltpu.SemaphoreType.DMA((S - 1,)),
        ],
        compiler_params=pltpu.CompilerParams(
            collective_id=0, has_side_effects=True, vmem_limit_bytes=40 * 1024 * 1024
        ),
        cost_estimate=pl.CostEstimate(flops=flops, bytes_accessed=1 << 20, transcendentals=0),
    )(station_data, jnp.transpose(template_waves, (1, 2, 0, 3)), channel_mask, pick_station, pick_lag)
    return result.T


def solution(mesh):
    in_specs = (
        P(None, ("sta", "tpl"), None),
        P(None, "sta"),
        P("tpl", "sta", None, None),
        P("tpl", None),
        P("tpl", None),
    )
    out_specs = P("sta", "tpl")
    run = functools.partial(body, mesh.shape["sta"], mesh.shape["tpl"])
    return jax.shard_map(run, mesh=mesh, in_specs=in_specs, out_specs=out_specs, check_vma=False)
```

```python
import functools

import jax
import jax.numpy as jnp
from jax import lax
from jax.experimental import pallas as pl
from jax.experimental.pallas import tpu as pltpu
from jax.sharding import PartitionSpec as P

NT = 1536
L = 640
LAGS = 1024
W = 128
EPS = 1e-05
MESH = pl.DeviceIdType.MESH
F32 = jnp.float32
BF16 = jnp.bfloat16

WL = L // W


def kernel(
    dims,
    data_hbm,
    waves_hbm,
    mask_hbm,
    ps_hbm,
    pl_hbm,
    out_ref,
    data_ref,
    waves_ref,
    mask_ref,
    ps_ref,
    pl_ref,
    buf0,
    buf1,
    buf2,
    s1_ref,
    s2_ref,
    sc_ref,
    tmp_ref,
    x4_ref,
    s4_ref,
    uw_ref,
    pkt_ref,
    pk_ref,
    toe_ref,
    acc_ref,
    part_ref,
    land_ref,
    row_tab,
    b_tab,
    st_tab,
    tp_tab,
    l_sem,
    d_send,
    d_recv,
    p_send,
    p_recv,
    r_send,
    r_recv,
):
    S, N, SL, G, CAP, RPS, RG, ND, STEP = dims
    X = N // 2
    NS = S * CAP
    H = W // STEP
    MR = NT // STEP
    KB = -(-(L + 2 * STEP - 2) // W)
    TPG = W // STEP
    NG = G // TPG
    RD = ND // STEP
    bufs = (buf0, buf1, buf2)
    me = lax.axis_index("sta")
    g = lax.axis_index("tpl")
    core = lax.rem(g, 2)
    xpos = g // 2
    mate = g + 1 - 2 * core
    peers = [{"sta": me, "tpl": mate}]
    far = []
    for k in range(1, X):
        far.append(lax.rem(xpos + k, X) * 2 + core)
        peers.append({"sta": me, "tpl": far[-1]})
    for k in range(1, S):
        peers.append({"sta": lax.rem(me + k, S), "tpl": g})

    local = [
        pltpu.make_async_copy(source, target, l_sem.at[i])
        for i, (source, target) in enumerate(
            [
                (data_hbm, data_ref),
                (waves_hbm, waves_ref),
                (ps_hbm, ps_ref),
                (pl_hbm, pl_ref),
                (mask_hbm, mask_ref),
            ]
        )
    ]
    for copy in local:
        copy.start()

    barrier = pltpu.get_barrier_semaphore()
    for peer in peers:
        pl.semaphore_signal(barrier, inc=1, device_id=peer, device_id_type=MESH)

    local[0].wait()
    own_row = pl.multiple_of(g * RG, 8)
    for c in range(3):
        bufs[c][pl.ds(N * RG, 16), :] = jnp.zeros((16, W), F32)
        bufs[c][pl.ds(own_row + RG - 8, 8), :] = jnp.zeros((8, W), F32)
        for b in range(RPS):
            bufs[c][pl.ds(own_row + b, SL, stride=RPS), :] = data_ref[c, :, b * W : (b + 1) * W]

    local[1].wait()
    for c in range(3):
        values = waves_ref[0, c].astype(F32)
        centred = values - jnp.mean(values, axis=-1, keepdims=True)
        spread = jnp.sqrt(jnp.mean(centred * centred, axis=-1, keepdims=True) + EPS)
        unit = centred / spread
        for a in range(WL):
            uw_ref[:, 3 * a + c, :] = unit[:, a * W : (a + 1) * W]

    def record_copy(c, kind):
        if kind == 0:
            source, target = g, mate
        elif kind < X:
            source, target = g, far[kind - 1]
        else:
            source, target = lax.rem(xpos + X - (kind - X + 1), X) * 2 + core, mate
        rows = pl.ds(pl.multiple_of(source * RG, 8), RG)
        return pltpu.make_async_remote_copy(
            src_ref=bufs[c].at[rows],
            dst_ref=bufs[c].at[rows],
            send_sem=d_send.at[c, kind],
            recv_sem=d_recv.at[c, kind],
            device_id={"sta": me, "tpl": target},
            device_id_type=MESH,
        )

    pl.semaphore_wait(barrier, len(peers))
    for c in range(3):
        for kind in list(range(1, X)) + [0]:
            record_copy(c, kind).start()

    for copy in local[2:]:
        copy.wait()

    def packet_step(d, _):
        count = jnp.int32(0)
        chosen = [jnp.int32(0)] * CAP
        low = d * SL * N
        for t in range(G):
            station = ps_ref[t, me]
            mine = jnp.logical_and(station >= low, station < low + SL * N).astype(jnp.int32)
            for j in range(CAP):
                chosen[j] = jnp.where(mine * (count + 1) == j + 1, t, chosen[j])
            count = count + mine
        for j in range(CAP):
            row = pl.multiple_of((d * CAP + j) * 16, 16)
            pkt_ref[pl.ds(row, 16), :] = uw_ref[chosen[j]].astype(BF16)
        return 0

    lax.fori_loop(0, S, packet_step, 0)

    def packet_copy(k):
        target = lax.rem(me + k, S)
        return pltpu.make_async_remote_copy(
            src_ref=pkt_ref.at[pl.ds(pl.multiple_of(target * CAP * 16, 16), CAP * 16)],
            dst_ref=pk_ref.at[pl.ds(pl.multiple_of(me * CAP * 16, 16), CAP * 16)],
            send_sem=p_send.at[k - 1],
            recv_sem=p_recv.at[k - 1],
            device_id={"sta": target, "tpl": g},
            device_id_type=MESH,
        )

    for k in range(1, S):
        packet_copy(k).start()
    own_packet = pl.ds(pl.multiple_of(me * CAP * 16, 16), CAP * 16)
    pk_ref[own_packet, :] = pkt_ref[own_packet, :]

    def table_step(p, _):
        count = jnp.int32(0)
        stations = [jnp.int32(0)] * CAP
        lags = [jnp.int32(0)] * CAP
        low = me * SL * N
        for t in range(G):
            station = ps_ref[t, p]
            lag = pl_ref[t, p]
            mine = jnp.logical_and(station >= low, station < low + SL * N).astype(jnp.int32)
            tp_tab[t * S + p] = jnp.where(mine == 1, p * CAP + jnp.minimum(count, CAP - 1), NS)
            for j in range(CAP):
                here = mine * (count + 1) == j + 1
                stations[j] = jnp.where(here, station - low, stations[j])
                lags[j] = jnp.where(here, lag, lags[j])
            count = count + mine
        for j in range(CAP):
            holder = stations[j] // SL
            first = holder * RG + (stations[j] - holder * SL) * RPS
            row_tab[p * CAP + j] = first * H + lags[j] // STEP
            b_tab[p * CAP + j] = lax.rem(lags[j], STEP)
            st_tab[p * CAP + j] = stations[j]
        return 0

    lax.fori_loop(0, S, table_step, 0)

    lane = lax.broadcasted_iota(jnp.int32, (8, W), 1)
    sub = lax.broadcasted_iota(jnp.int32, (8, W), 0)
    ones_k = lax.broadcasted_iota(jnp.int32, (2 * W, W), 0)
    ones_r = lax.broadcasted_iota(jnp.int32, (2 * W, W), 1)
    window = jnp.logical_and(ones_k >= ones_r, ones_k < ones_r + W).astype(F32).astype(BF16)

    def window_sum(values):
        high = values.astype(BF16)
        rest = values - high.astype(F32)
        middle = rest.astype(BF16)
        low = (rest - middle.astype(F32)).astype(BF16)
        total = jnp.dot(low, window, preferred_element_type=F32)
        total += jnp.dot(middle, window, preferred_element_type=F32)
        return total + jnp.dot(high, window, preferred_element_type=F32)

    tail = pl.ds(N * RG, 16)
    s1_ref[tail, :] = jnp.zeros((16, W), F32)
    s2_ref[tail, :] = jnp.zeros((16, W), F32)
    sc_ref[tail, :] = jnp.zeros((16, W), F32)
    acc_ref[NS] = jnp.zeros((MR, STEP), F32)

    def scales_of(buf):
        def sums(h, _):
            row = pl.multiple_of(h * RG, 8)
            x = jnp.concatenate([buf[pl.ds(row, RG), :], buf[pl.ds(row + 1, RG), :]], axis=1)
            s1_ref[pl.ds(row, RG), :] = window_sum(x)
            s2_ref[pl.ds(row, RG), :] = window_sum(x * x)
            return 0

        lax.fori_loop(0, N, sums, 0)

        def finish(h, _):
            row = pl.multiple_of(h * RG, 8)
            one = s1_ref[pl.ds(row, RG), :]
            two = s2_ref[pl.ds(row, RG), :]
            for a in range(1, WL):
                one += s1_ref[pl.ds(row + a, RG), :]
                two += s2_ref[pl.ds(row + a, RG), :]
            one = one * (1.0 / L)
            two = two * (1.0 / L)
            sc_ref[pl.ds(row, RG), :] = lax.rsqrt(two - one * one + EPS) * (1.0 / L)
            return 0

        lax.fori_loop(0, N, finish, 0)

    def shifted_rows(source, target):
        def step(h, _):
            row = pl.multiple_of(h * RG, 8)
            for q in range(1, H):
                whole = source[pl.ds(row, RG + 8), :]
                tmp_ref[q - 1] = pltpu.roll(whole, W - STEP * q, axis=1)
            target[pl.ds(row * H, RG, stride=H), :] = source[pl.ds(row, RG), :]
            wide = lax.broadcasted_iota(jnp.int32, (RG, W), 1)
            for q in range(1, H):
                now = tmp_ref[q - 1, pl.ds(0, RG), :]
                after = tmp_ref[q - 1, pl.ds(1, RG), :]
                target[pl.ds(row * H + q, RG, stride=H), :] = jnp.where(
                    wide < W - STEP * q, now, after
                )
            return 0

        lax.fori_loop(0, N, step, 0)

    def toeplitz_step(slot, _):
        shift = b_tab[slot]
        unit = pk_ref[pl.ds(pl.multiple_of(slot * 16, 16), 16), :].astype(F32)
        unit = pltpu.roll(unit, shift, axis=1)
        zero_tile = jnp.zeros((8, W), F32)
        for c in range(3):
            rows = [
                jnp.broadcast_to(unit[3 * a + c : 3 * a + c + 1], (8, W)) for a in range(WL)
            ]
            strips = []
            for j in range(STEP // 8):
                turned = [
                    pltpu.roll(v, 8 * j, axis=1, stride=1, stride_axis=0) for v in rows
                ]
                turned = [zero_tile] + turned + [zero_tile]
                keep = lane >= sub + (8 * j + shift)
                strips.append(
                    jnp.concatenate(
                        [jnp.where(keep, turned[a + 1], turned[a]) for a in range(KB)], axis=1
                    )
                )
            toe_ref[slot * 3 + c] = jnp.concatenate(strips, axis=0).astype(BF16)
        return 0

    def slots_of(c):
        def slot_step(slot, _):
            row = row_tab[slot]
            shift = b_tab[slot]
            weight = mask_ref[c, st_tab[slot]].astype(F32)
            frames = jnp.concatenate(
                [x4_ref[pl.ds(row + H * a, MR), :] for a in range(KB)], axis=1
            ).astype(BF16)
            corr = lax.dot_general(
                frames, toe_ref[slot * 3 + c], (((1,), (1,)), ((), ())), preferred_element_type=F32
            )
            factor = pltpu.roll(s4_ref[pl.ds(row, MR), :], lax.rem(W - shift, W), axis=1)
            term = corr * (factor[:, :STEP] * weight)
            if c == 0:
                acc_ref[slot] = term
            else:
                acc_ref[slot] += term
            return 0

        lax.fori_loop(0, NS, slot_step, 0, unroll=4)

    def pass_on(c):
        for kind in range(1, X):
            record_copy(c, kind).wait_recv()
            record_copy(c, X - 1 + kind).start()

    pass_on(0)
    for k in range(1, S):
        packet_copy(k).wait_recv()
    lax.fori_loop(0, NS, toeplitz_step, 0, unroll=2)
    for c in range(3):
        record_copy(c, 0).wait_recv()
        for kind in range(X, 2 * X - 1):
            record_copy(c, kind).wait_recv()
        if c < 2:
            pass_on(c + 1)
        shifted_rows(bufs[c], x4_ref)
        scales_of(bufs[c])
        shifted_rows(sc_ref, s4_ref)
        slots_of(c)

    for group in range(NG):
        sums = []
        for t in range(group * TPG, (group + 1) * TPG):

            def add_pick(p, total):
                return total + acc_ref[tp_tab[t * S + p]]

            sums.append(lax.fori_loop(0, S, add_pick, jnp.zeros((MR, STEP), F32), unroll=8))
        side = jnp.concatenate(sums, axis=1)
        for d in range(S):
            part_ref[d, group, pl.ds(0, RD), :] = side[RD * d : RD * (d + 1)]

    def sum_copy(k):
        target = lax.rem(me + k, S)
        return pltpu.make_async_remote_copy(
            src_ref=part_ref.at[target],
            dst_ref=land_ref.at[k - 1],
            send_sem=r_send.at[k - 1],
            recv_sem=r_recv.at[k - 1],
            device_id={"sta": target, "tpl": g},
            device_id_type=MESH,
        )

    for k in range(1, S):
        sum_copy(k).start()
    total = part_ref[me]
    for k in range(1, S):
        sum_copy(k).wait_recv()
        total = total + land_ref[k - 1]
    for t in range(G):
        m = t % TPG
        for r in range(RD):
            out_ref[t : t + 1, STEP * r : STEP * (r + 1)] = total[
                t // TPG, r : r + 1, STEP * m : STEP * (m + 1)
            ]

    for c in range(3):
        for kind in range(2 * X - 1):
            record_copy(c, kind).wait_send()
    for k in range(1, S):
        packet_copy(k).wait_send()
        sum_copy(k).wait_send()


def body(S, N, station_data, channel_mask, template_waves, pick_station, pick_lag):
    SL, samples = station_data.shape[1], station_data.shape[2]
    G, picks = pick_station.shape
    assert picks == S and template_waves.shape[1] == 1
    CAP = max(2, G // 8)
    RPS = samples // W
    RG = -(-(SL * RPS) // 8) * 8
    ND = NT // S
    STEP = 32 if ND % 32 == 0 else 16
    H = W // STEP
    MR = NT // STEP
    KB = -(-(L + 2 * STEP - 2) // W)
    RDP = -(-(ND // STEP) // 8) * 8
    NG = G * STEP // W
    X = N // 2
    NS = S * CAP
    dims = (S, N, SL, G, CAP, RPS, RG, ND, STEP)
    rows = N * RG + 16
    vmem = pl.BlockSpec(memory_space=pltpu.VMEM)
    hbm = pl.BlockSpec(memory_space=pltpu.HBM)
    flops = 2 * NS * 3 * MR * STEP * KB * W
    result = pl.pallas_call(
        functools.partial(kernel, dims),
        out_shape=jax.ShapeDtypeStruct((G, ND), F32),
        in_specs=[hbm] * 5,
        out_specs=vmem,
        scratch_shapes=[
            pltpu.VMEM(station_data.shape, F32),
            pltpu.VMEM((1, 3, G, L), BF16),
            pltpu.SMEM(channel_mask.shape, jnp.int32),
            pltpu.SMEM(pick_station.shape, jnp.int32),
            pltpu.SMEM(pick_lag.shape, jnp.int32),
            pltpu.VMEM((rows, W), F32),
            pltpu.VMEM((rows, W), F32),
            pltpu.VMEM((rows, W), F32),
            pltpu.VMEM((rows, W), F32),
            pltpu.VMEM((rows, W), F32),
            pltpu.VMEM((rows, W), F32),
            pltpu.VMEM((H - 1, RG + 8, W), F32),
            pltpu.VMEM((rows * H, W), F32),
            pltpu.VMEM((rows * H, W), F32),
            pltpu.VMEM((G, 16, W), F32),
            pltpu.VMEM((NS * 16, W), BF16),
            pltpu.VMEM((NS * 16, W), BF16),
            pltpu.VMEM((NS * 3, STEP, KB * W), BF16),
            pltpu.VMEM((NS + 1, MR, STEP), F32),
            pltpu.VMEM((S, NG, RDP, W), F32),
            pltpu.VMEM((S - 1, NG, RDP, W), F32),
            pltpu.SMEM((NS,), jnp.int32),
            pltpu.SMEM((NS,), jnp.int32),
            pltpu.SMEM((NS,), jnp.int32),
            pltpu.SMEM((G * S,), jnp.int32),
            pltpu.SemaphoreType.DMA((5,)),
            pltpu.SemaphoreType.DMA((3, 2 * X - 1)),
            pltpu.SemaphoreType.DMA((3, 2 * X - 1)),
            pltpu.SemaphoreType.DMA((S - 1,)),
            pltpu.SemaphoreType.DMA((S - 1,)),
            pltpu.SemaphoreType.DMA((S - 1,)),
            pltpu.SemaphoreType.DMA((S - 1,)),
        ],
        compiler_params=pltpu.CompilerParams(
            collective_id=0, has_side_effects=True, vmem_limit_bytes=40 * 1024 * 1024
        ),
        cost_estimate=pl.CostEstimate(flops=flops, bytes_accessed=1 << 20, transcendentals=0),
    )(station_data, jnp.transpose(template_waves, (1, 2, 0, 3)), channel_mask, pick_station, pick_lag)
    return result.T


def solution(mesh):
    in_specs = (
        P(None, ("sta", "tpl"), None),
        P(None, "sta"),
        P("tpl", "sta", None, None),
        P("tpl", None),
        P("tpl", None),
    )
    out_specs = P("sta", "tpl")
    run = functools.partial(body, mesh.shape["sta"], mesh.shape["tpl"])
    return jax.shard_map(run, mesh=mesh, in_specs=in_specs, out_specs=out_specs, check_vma=False)
```

```python
import functools

import jax
import jax.numpy as jnp
from jax import lax
from jax.experimental import pallas as pl
from jax.experimental.pallas import tpu as pltpu
from jax.sharding import PartitionSpec as P

NT = 1536
L = 640
LAGS = 1024
W = 128
EPS = 1e-05
MESH = pl.DeviceIdType.MESH
F32 = jnp.float32
BF16 = jnp.bfloat16

WL = L // W


def kernel(
    dims,
    data_hbm,
    waves_hbm,
    mask_hbm,
    ps_hbm,
    pl_hbm,
    out_ref,
    data_ref,
    waves_ref,
    mask_ref,
    ps_ref,
    pl_ref,
    buf0,
    buf1,
    buf2,
    d2_ref,
    tot_ref,
    sc_ref,
    x4_ref,
    s4_ref,
    uw_ref,
    pkt_ref,
    pk_ref,
    toe_ref,
    acc_ref,
    part_ref,
    land_ref,
    row_tab,
    b_tab,
    st_tab,
    tp_tab,
    l_sem,
    d_send,
    d_recv,
    p_send,
    p_recv,
    r_send,
    r_recv,
):
    S, N, SL, G, CAP, RPS, RG, ND, STEP = dims
    X = N // 2
    NS = S * CAP
    H = W // STEP
    MR = NT // STEP
    KB = -(-(L + 2 * STEP - 2) // W)
    TPG = W // STEP
    NG = G // TPG
    RD = ND // STEP
    PK = 8 // RD
    RE = RG + 8
    bufs = (buf0, buf1, buf2)
    me = lax.axis_index("sta")
    g = lax.axis_index("tpl")
    core = lax.rem(g, 2)
    xpos = g // 2
    mate = g + 1 - 2 * core
    peers = [{"sta": me, "tpl": mate}]
    far = []
    for k in range(1, X):
        far.append(lax.rem(xpos + k, X) * 2 + core)
        peers.append({"sta": me, "tpl": far[-1]})
    for k in range(1, S):
        peers.append({"sta": lax.rem(me + k, S), "tpl": g})

    local = [
        pltpu.make_async_copy(source, target, l_sem.at[i])
        for i, (source, target) in enumerate(
            [
                (data_hbm, data_ref),
                (waves_hbm, waves_ref),
                (ps_hbm, ps_ref),
                (pl_hbm, pl_ref),
                (mask_hbm, mask_ref),
            ]
        )
    ]
    for copy in local:
        copy.start()

    barrier = pltpu.get_barrier_semaphore()
    for peer in peers:
        pl.semaphore_signal(barrier, inc=1, device_id=peer, device_id_type=MESH)

    local[0].wait()
    for c in range(3):
        bufs[c][g, pl.ds(RG - 8, 8), :] = jnp.zeros((8, W), F32)
        for h in range(N):
            bufs[c][h, pl.ds(RG, 8), :] = jnp.zeros((8, W), F32)
        sc_ref[c, pl.ds(RG, 8), :] = jnp.zeros((8, W), F32)
        for b in range(RPS):
            bufs[c][g, pl.ds(b, SL, stride=RPS), :] = data_ref[c, :, b * W : (b + 1) * W]
    acc_ref[NS] = jnp.zeros((MR, STEP), F32)

    local[1].wait()
    for c in range(3):
        values = waves_ref[0, c].astype(F32)
        centred = values - jnp.mean(values, axis=-1, keepdims=True)
        spread = jnp.sqrt(jnp.mean(centred * centred, axis=-1, keepdims=True) + EPS)
        unit = centred / spread
        for a in range(WL):
            uw_ref[:, 3 * a + c, :] = unit[:, a * W : (a + 1) * W]

    def record_copy(c, kind):
        if kind == 0:
            source, target = g, mate
        elif kind < X:
            source, target = g, far[kind - 1]
        else:
            source, target = lax.rem(xpos + X - (kind - X + 1), X) * 2 + core, mate
        return pltpu.make_async_remote_copy(
            src_ref=bufs[c].at[source, pl.ds(0, RG)],
            dst_ref=bufs[c].at[source, pl.ds(0, RG)],
            send_sem=d_send.at[c, kind],
            recv_sem=d_recv.at[c, kind],
            device_id={"sta": me, "tpl": target},
            device_id_type=MESH,
        )

    pl.semaphore_wait(barrier, len(peers))
    for c in range(3):
        for kind in list(range(1, X)) + [0]:
            record_copy(c, kind).start()

    for copy in local[2:]:
        copy.wait()

    def packet_step(d, _):
        count = jnp.int32(0)
        chosen = [jnp.int32(0)] * CAP
        low = d * SL * N
        for t in range(G):
            station = ps_ref[t, me]
            mine = jnp.logical_and(station >= low, station < low + SL * N).astype(jnp.int32)
            for j in range(CAP):
                chosen[j] = jnp.where(mine * (count + 1) == j + 1, t, chosen[j])
            count = count + mine
        for j in range(CAP):
            row = pl.multiple_of((d * CAP + j) * 16, 16)
            pkt_ref[pl.ds(row, 16), :] = uw_ref[chosen[j]].astype(BF16)
        return 0

    lax.fori_loop(0, S, packet_step, 0)

    def packet_copy(k):
        target = lax.rem(me + k, S)
        return pltpu.make_async_remote_copy(
            src_ref=pkt_ref.at[pl.ds(pl.multiple_of(target * CAP * 16, 16), CAP * 16)],
            dst_ref=pk_ref.at[pl.ds(pl.multiple_of(me * CAP * 16, 16), CAP * 16)],
            send_sem=p_send.at[k - 1],
            recv_sem=p_recv.at[k - 1],
            device_id={"sta": target, "tpl": g},
            device_id_type=MESH,
        )

    for k in range(1, S):
        packet_copy(k).start()
    own_packet = pl.ds(pl.multiple_of(me * CAP * 16, 16), CAP * 16)
    pk_ref[own_packet, :] = pkt_ref[own_packet, :]

    def table_step(p, _):
        count = jnp.int32(0)
        stations = [jnp.int32(0)] * CAP
        lags = [jnp.int32(0)] * CAP
        low = me * SL * N
        for t in range(G):
            station = ps_ref[t, p]
            lag = pl_ref[t, p]
            mine = jnp.logical_and(station >= low, station < low + SL * N).astype(jnp.int32)
            tp_tab[t * S + p] = jnp.where(mine == 1, p * CAP + jnp.minimum(count, CAP - 1), NS)
            for j in range(CAP):
                here = mine * (count + 1) == j + 1
                stations[j] = jnp.where(here, station - low, stations[j])
                lags[j] = jnp.where(here, lag, lags[j])
            count = count + mine
        for j in range(CAP):
            holder = stations[j] // SL
            first = holder * RG + (stations[j] - holder * SL) * RPS
            row_tab[p * CAP + j] = first * H + lags[j] // STEP
            b_tab[p * CAP + j] = lax.rem(lags[j], STEP)
            st_tab[p * CAP + j] = stations[j]
        return 0

    lax.fori_loop(0, S, table_step, 0)

    lane = lax.broadcasted_iota(jnp.int32, (8, W), 1)
    sub = lax.broadcasted_iota(jnp.int32, (8, W), 0)
    ones_k = lax.broadcasted_iota(jnp.int32, (W, 2 * W), 0)
    ones_r = lax.broadcasted_iota(jnp.int32, (W, 2 * W), 1)
    window = jnp.logical_and(ones_k >= ones_r, ones_r < W)
    window = jnp.logical_or(window, ones_k < ones_r - W).astype(F32).astype(BF16)

    def edge_sums(values):
        high = values.astype(BF16)
        rest = values - high.astype(F32)
        middle = rest.astype(BF16)
        low = (rest - middle.astype(F32)).astype(BF16)
        total = jnp.dot(low, window, preferred_element_type=F32)
        total += jnp.dot(middle, window, preferred_element_type=F32)
        return total + jnp.dot(high, window, preferred_element_type=F32)

    def shifted_rows(source, target, c, h):
        wide = lax.broadcasted_iota(jnp.int32, (RG, W), 1)
        now = source[pl.ds(0, RG), :]
        after = source[pl.ds(1, RG), :]
        row = h * (RG * H)
        target[c, pl.ds(row, RG, stride=H), :] = now
        for q in range(1, H):
            target[c, pl.ds(row + q, RG, stride=H), :] = jnp.where(
                wide < W - STEP * q,
                pltpu.roll(now, W - STEP * q, axis=1),
                pltpu.roll(after, W - STEP * q, axis=1),
            )

    def prepare(c, h):
        buf = bufs[c].at[h]
        shifted_rows(buf, x4_ref, c, h)
        x = buf[...]
        means = []
        for q, values in enumerate((x, x * x)):
            edges = edge_sums(values)
            d2_ref[c, q] = edges[:, W:]
            tot_ref[c, q] = edges[:, :W] + edges[:, W:]
            total = edges[:RG, :W] + d2_ref[c, q, pl.ds(WL, RG), :]
            for a in range(1, WL):
                total += tot_ref[c, q, pl.ds(a, RG), :]
            means.append(total * (1.0 / L))
        one, two = means
        sc_ref[c, pl.ds(0, RG), :] = lax.rsqrt(two - one * one + EPS) * (1.0 / L)
        shifted_rows(sc_ref.at[c], s4_ref, c, h)

    def toeplitz_step(slot, _):
        shift = b_tab[slot]
        unit = pk_ref[pl.ds(pl.multiple_of(slot * 16, 16), 16), :].astype(F32)
        unit = pltpu.roll(unit, shift, axis=1)
        zero_tile = jnp.zeros((8, W), F32)
        for c in range(3):
            rows = [
                jnp.broadcast_to(unit[3 * a + c : 3 * a + c + 1], (8, W)) for a in range(WL)
            ]
            for j in range(0, STEP // 8, 2):
                strips = []
                for i in (j, j + 1):
                    turned = [
                        pltpu.roll(v, 8 * i, axis=1, stride=1, stride_axis=0) for v in rows
                    ]
                    turned = [zero_tile] + turned + [zero_tile]
                    keep = lane >= sub + (8 * i + shift)
                    strips.append(
                        jnp.concatenate(
                            [jnp.where(keep, turned[a + 1], turned[a]) for a in range(KB)], axis=1
                        )
                    )
                toe_ref[slot * 3 + c, pl.ds(8 * j, 16), :] = jnp.concatenate(
                    strips, axis=0
                ).astype(BF16)
        return 0

    def slot_step(slot, _):
        row = row_tab[slot]
        shift = b_tab[slot]
        back = lax.rem(W - shift, W)
        terms = []
        for c in range(3):
            weight = mask_ref[c, st_tab[slot]].astype(F32)
            frames = jnp.concatenate(
                [x4_ref[c, pl.ds(row + H * a, MR), :] for a in range(KB)], axis=1
            ).astype(BF16)
            corr = lax.dot_general(
                frames, toe_ref[slot * 3 + c], (((1,), (1,)), ((), ())), preferred_element_type=F32
            )
            factor = pltpu.roll(s4_ref[c, pl.ds(row, MR), :], back, axis=1)
            terms.append(corr * (factor[:, :STEP] * weight))
        acc_ref[slot] = terms[0] + terms[1] + terms[2]
        return 0

    def pass_on(c):
        for kind in range(1, X):
            record_copy(c, kind).wait_recv()
            record_copy(c, X - 1 + kind).start()

    for c in range(3):
        prepare(c, g)
    pass_on(0)
    for k in range(1, S):
        packet_copy(k).wait_recv()
    lax.fori_loop(0, NS, toeplitz_step, 0, unroll=2)
    pass_on(1)
    pass_on(2)
    for c in range(3):
        record_copy(c, 0).wait_recv()
        prepare(c, mate)
    for k in range(1, X):
        for c in range(3):
            prepare(c, lax.rem(xpos + X - k, X) * 2 + core)
    for k in range(1, X):
        for c in range(3):
            record_copy(c, X - 1 + k).wait_recv()
            prepare(c, lax.rem(xpos + X - k, X) * 2 + 1 - core)
    lax.fori_loop(0, NS, slot_step, 0, unroll=2)

    for group in range(NG):
        sums = []
        for t in range(group * TPG, (group + 1) * TPG):

            def add_pick(p, total):
                return total + acc_ref[tp_tab[t * S + p]]

            sums.append(lax.fori_loop(0, S, add_pick, jnp.zeros((MR, STEP), F32), unroll=8))
        side = jnp.concatenate(sums, axis=1)
        for d in range(S):
            part_ref[d, group // PK, pl.ds(group % PK * RD, RD), :] = side[RD * d : RD * (d + 1)]

    def sum_copy(k):
        target = lax.rem(me + k, S)
        return pltpu.make_async_remote_copy(
            src_ref=part_ref.at[target],
            dst_ref=land_ref.at[k - 1],
            send_sem=r_send.at[k - 1],
            recv_sem=r_recv.at[k - 1],
            device_id={"sta": target, "tpl": g},
            device_id_type=MESH,
        )

    for k in range(1, S):
        sum_copy(k).start()
    total = part_ref[me]
    for k in range(1, S):
        sum_copy(k).wait_recv()
        total = total + land_ref[k - 1]
    for t in range(G):
        m = t % TPG
        low = t // TPG % PK * RD
        for r in range(RD):
            out_ref[t : t + 1, STEP * r : STEP * (r + 1)] = total[
                t // TPG // PK, low + r : low + r + 1, STEP * m : STEP * (m + 1)
            ]

    for c in range(3):
        for kind in range(2 * X - 1):
            record_copy(c, kind).wait_send()
    for k in range(1, S):
        packet_copy(k).wait_send()
        sum_copy(k).wait_send()


def body(S, N, station_data, channel_mask, template_waves, pick_station, pick_lag):
    SL, samples = station_data.shape[1], station_data.shape[2]
    G, picks = pick_station.shape
    assert picks == S and template_waves.shape[1] == 1
    CAP = max(2, G // 8)
    RPS = samples // W
    RG = -(-(SL * RPS) // 8) * 8
    ND = NT // S
    STEP = 64 if ND % 64 == 0 else 16
    H = W // STEP
    MR = NT // STEP
    KB = -(-(L + 2 * STEP - 2) // W)
    PK = 8 // (ND // STEP)
    NP = -(-(G * STEP // W) // PK)
    X = N // 2
    NS = S * CAP
    dims = (S, N, SL, G, CAP, RPS, RG, ND, STEP)
    rows = N * RG * H
    vmem = pl.BlockSpec(memory_space=pltpu.VMEM)
    hbm = pl.BlockSpec(memory_space=pltpu.HBM)
    flops = 2 * NS * 3 * MR * STEP * KB * W
    result = pl.pallas_call(
        functools.partial(kernel, dims),
        out_shape=jax.ShapeDtypeStruct((G, ND), F32),
        in_specs=[hbm] * 5,
        out_specs=vmem,
        scratch_shapes=[
            pltpu.VMEM(station_data.shape, F32),
            pltpu.VMEM((1, 3, G, L), BF16),
            pltpu.SMEM(channel_mask.shape, jnp.int32),
            pltpu.SMEM(pick_station.shape, jnp.int32),
            pltpu.SMEM(pick_lag.shape, jnp.int32),
            pltpu.VMEM((N, RG + 8, W), F32),
            pltpu.VMEM((N, RG + 8, W), F32),
            pltpu.VMEM((N, RG + 8, W), F32),
            pltpu.VMEM((3, 2, RG + 8, W), F32),
            pltpu.VMEM((3, 2, RG + 8, W), F32),
            pltpu.VMEM((3, RG + 8, W), F32),
            pltpu.VMEM((3, rows, W), F32),
            pltpu.VMEM((3, rows, W), F32),
            pltpu.VMEM((G, 16, W), F32),
            pltpu.VMEM((NS * 16, W), BF16),
            pltpu.VMEM((NS * 16, W), BF16),
            pltpu.VMEM((NS * 3, STEP, KB * W), BF16),
            pltpu.VMEM((NS + 1, MR, STEP), F32),
            pltpu.VMEM((S, NP, 8, W), F32),
            pltpu.VMEM((S - 1, NP, 8, W), F32),
            pltpu.SMEM((NS,), jnp.int32),
            pltpu.SMEM((NS,), jnp.int32),
            pltpu.SMEM((NS,), jnp.int32),
            pltpu.SMEM((G * S,), jnp.int32),
            pltpu.SemaphoreType.DMA((5,)),
            pltpu.SemaphoreType.DMA((3, 2 * X - 1)),
            pltpu.SemaphoreType.DMA((3, 2 * X - 1)),
            pltpu.SemaphoreType.DMA((S - 1,)),
            pltpu.SemaphoreType.DMA((S - 1,)),
            pltpu.SemaphoreType.DMA((S - 1,)),
            pltpu.SemaphoreType.DMA((S - 1,)),
        ],
        compiler_params=pltpu.CompilerParams(
            collective_id=0, has_side_effects=True, vmem_limit_bytes=63 * 1024 * 1024
        ),
        cost_estimate=pl.CostEstimate(flops=flops, bytes_accessed=1 << 20, transcendentals=0),
    )(station_data, jnp.transpose(template_waves, (1, 2, 0, 3)), channel_mask, pick_station, pick_lag)
    return result.T


def solution(mesh):
    in_specs = (
        P(None, ("sta", "tpl"), None),
        P(None, "sta"),
        P("tpl", "sta", None, None),
        P("tpl", None),
        P("tpl", None),
    )
    out_specs = P("sta", "tpl")
    run = functools.partial(body, mesh.shape["sta"], mesh.shape["tpl"])
    return jax.shard_map(run, mesh=mesh, in_specs=in_specs, out_specs=out_specs, check_vma=False)
```

```python
import functools

import jax
import jax.numpy as jnp
from jax import lax
from jax.experimental import pallas as pl
from jax.experimental.pallas import tpu as pltpu
from jax.sharding import PartitionSpec as P

NT = 1536
L = 640
LAGS = 1024
W = 128
EPS = 1e-05
MESH = pl.DeviceIdType.MESH
F32 = jnp.float32
BF16 = jnp.bfloat16

WL = L // W


def kernel(
    dims,
    data_hbm,
    waves_hbm,
    mask_hbm,
    ps_hbm,
    pl_hbm,
    out_ref,
    data_ref,
    waves_ref,
    mask_ref,
    ps_ref,
    pl_ref,
    buf0,
    buf1,
    buf2,
    d1_ref,
    d2_ref,
    tot_ref,
    sc_ref,
    x4_ref,
    s4_ref,
    uw_ref,
    pkt_ref,
    pk_ref,
    toe_ref,
    acc_ref,
    part_ref,
    land_ref,
    row_tab,
    b_tab,
    st_tab,
    tp_tab,
    l_sem,
    d_send,
    d_recv,
    p_send,
    p_recv,
    r_send,
    r_recv,
):
    S, N, SL, G, CAP, RPS, RG, ND, STEP = dims
    X = N // 2
    NS = S * CAP
    H = W // STEP
    MR = NT // STEP
    KB = -(-(L + 2 * STEP - 2) // W)
    TPG = W // STEP
    NG = G // TPG
    RD = ND // STEP
    PK = 8 // RD
    bufs = (buf0, buf1, buf2)
    me = lax.axis_index("sta")
    g = lax.axis_index("tpl")
    core = lax.rem(g, 2)
    xpos = g // 2
    mate = g + 1 - 2 * core
    peers = [{"sta": me, "tpl": mate}]
    far = []
    for k in range(1, X):
        far.append(lax.rem(xpos + k, X) * 2 + core)
        peers.append({"sta": me, "tpl": far[-1]})
    for k in range(1, S):
        peers.append({"sta": lax.rem(me + k, S), "tpl": g})

    local = [
        pltpu.make_async_copy(source, target, l_sem.at[i])
        for i, (source, target) in enumerate(
            [
                (data_hbm, data_ref),
                (waves_hbm, waves_ref),
                (ps_hbm, ps_ref),
                (pl_hbm, pl_ref),
                (mask_hbm, mask_ref),
            ]
        )
    ]
    for copy in local:
        copy.start()

    barrier = pltpu.get_barrier_semaphore()
    for peer in peers:
        pl.semaphore_signal(barrier, inc=1, device_id=peer, device_id_type=MESH)

    local[0].wait()
    for c in range(3):
        bufs[c][g, pl.ds(RG - 8, 8), :] = jnp.zeros((8, W), F32)
        for h in range(N):
            bufs[c][h, pl.ds(RG, 8), :] = jnp.zeros((8, W), F32)
        sc_ref[c, pl.ds(RG, 8), :] = jnp.zeros((8, W), F32)
        for b in range(RPS):
            bufs[c][g, pl.ds(b, SL, stride=RPS), :] = data_ref[c, :, b * W : (b + 1) * W]
    acc_ref[NS] = jnp.zeros((MR, STEP), F32)

    local[1].wait()
    for c in range(3):
        values = waves_ref[0, c].astype(F32)
        centred = values - jnp.mean(values, axis=-1, keepdims=True)
        spread = jnp.sqrt(jnp.mean(centred * centred, axis=-1, keepdims=True) + EPS)
        unit = centred / spread
        for a in range(WL):
            uw_ref[:, 3 * a + c, :] = unit[:, a * W : (a + 1) * W]

    def record_copy(c, kind):
        if kind == 0:
            source, target = g, mate
        elif kind < X:
            source, target = g, far[kind - 1]
        else:
            source, target = lax.rem(xpos + X - (kind - X + 1), X) * 2 + core, mate
        return pltpu.make_async_remote_copy(
            src_ref=bufs[c].at[source, pl.ds(0, RG)],
            dst_ref=bufs[c].at[source, pl.ds(0, RG)],
            send_sem=d_send.at[c, kind],
            recv_sem=d_recv.at[c, kind],
            device_id={"sta": me, "tpl": target},
            device_id_type=MESH,
        )

    pl.semaphore_wait(barrier, len(peers))
    for c in range(3):
        for kind in list(range(1, X)) + [0]:
            record_copy(c, kind).start()

    for copy in local[2:]:
        copy.wait()

    def packet_step(d, _):
        count = jnp.int32(0)
        chosen = [jnp.int32(0)] * CAP
        low = d * SL * N
        for t in range(G):
            station = ps_ref[t, me]
            mine = jnp.logical_and(station >= low, station < low + SL * N).astype(jnp.int32)
            for j in range(CAP):
                chosen[j] = jnp.where(mine * (count + 1) == j + 1, t, chosen[j])
            count = count + mine
        for j in range(CAP):
            row = pl.multiple_of((d * CAP + j) * 16, 16)
            pkt_ref[pl.ds(row, 16), :] = uw_ref[chosen[j]].astype(BF16)
        return 0

    lax.fori_loop(0, S, packet_step, 0)

    def packet_copy(k):
        target = lax.rem(me + k, S)
        return pltpu.make_async_remote_copy(
            src_ref=pkt_ref.at[pl.ds(pl.multiple_of(target * CAP * 16, 16), CAP * 16)],
            dst_ref=pk_ref.at[pl.ds(pl.multiple_of(me * CAP * 16, 16), CAP * 16)],
            send_sem=p_send.at[k - 1],
            recv_sem=p_recv.at[k - 1],
            device_id={"sta": target, "tpl": g},
            device_id_type=MESH,
        )

    for k in range(1, S):
        packet_copy(k).start()
    own_packet = pl.ds(pl.multiple_of(me * CAP * 16, 16), CAP * 16)
    pk_ref[own_packet, :] = pkt_ref[own_packet, :]

    def table_step(p, _):
        count = jnp.int32(0)
        stations = [jnp.int32(0)] * CAP
        lags = [jnp.int32(0)] * CAP
        low = me * SL * N
        for t in range(G):
            station = ps_ref[t, p]
            lag = pl_ref[t, p]
            mine = jnp.logical_and(station >= low, station < low + SL * N).astype(jnp.int32)
            tp_tab[t * S + p] = jnp.where(mine == 1, p * CAP + jnp.minimum(count, CAP - 1), NS)
            for j in range(CAP):
                here = mine * (count + 1) == j + 1
                stations[j] = jnp.where(here, station - low, stations[j])
                lags[j] = jnp.where(here, lag, lags[j])
            count = count + mine
        for j in range(CAP):
            holder = stations[j] // SL
            first = holder * RG + (stations[j] - holder * SL) * RPS
            row_tab[p * CAP + j] = first * H + lags[j] // STEP
            b_tab[p * CAP + j] = lax.rem(lags[j], STEP)
            st_tab[p * CAP + j] = stations[j]
        return 0

    lax.fori_loop(0, S, table_step, 0)

    lane = lax.broadcasted_iota(jnp.int32, (8, W), 1)
    sub = lax.broadcasted_iota(jnp.int32, (8, W), 0)
    ones_k = lax.broadcasted_iota(jnp.int32, (W, 2 * W), 0)
    ones_r = lax.broadcasted_iota(jnp.int32, (W, 2 * W), 1)
    window = jnp.logical_and(ones_k >= ones_r, ones_r < W)
    window = jnp.logical_or(window, ones_k < ones_r - W).astype(F32).astype(BF16)
    window = jnp.concatenate([window] * 3, axis=0)

    def edge_sums(values):
        high = values.astype(BF16)
        rest = values - high.astype(F32)
        middle = rest.astype(BF16)
        low = (rest - middle.astype(F32)).astype(BF16)
        parts = jnp.concatenate([low, middle, high], axis=1)
        return jnp.dot(parts, window, preferred_element_type=F32)

    def shifted_rows(source, target, c, h):
        wide = lax.broadcasted_iota(jnp.int32, (RG, W), 1)
        now = source[pl.ds(0, RG), :]
        after = source[pl.ds(1, RG), :]
        row = h * (RG * H)
        target[c, pl.ds(row, RG, stride=H), :] = now
        for q in range(1, H):
            target[c, pl.ds(row + q, RG, stride=H), :] = jnp.where(
                wide < W - STEP * q,
                pltpu.roll(now, W - STEP * q, axis=1),
                pltpu.roll(after, W - STEP * q, axis=1),
            )

    def prepare(h):
        for c in range(3):
            shifted_rows(bufs[c].at[h], x4_ref, c, h)
        x = jnp.concatenate([bufs[c][h] for c in range(3)], axis=0)
        edges = edge_sums(jnp.concatenate([x, x * x], axis=0))
        RE = RG + 8
        d1_ref[...] = edges[:, :W]
        d2_ref[...] = edges[:, W:]
        tot_ref[...] = edges[:, :W] + edges[:, W:]
        for c in range(3):
            means = []
            for q in range(2):
                at = (q * 3 + c) * RE
                total = d1_ref[pl.ds(at, RG), :] + d2_ref[pl.ds(at + WL, RG), :]
                for a in range(1, WL):
                    total += tot_ref[pl.ds(at + a, RG), :]
                means.append(total * (1.0 / L))
            one, two = means
            sc_ref[c, pl.ds(0, RG), :] = lax.rsqrt(two - one * one + EPS) * (1.0 / L)
            shifted_rows(sc_ref.at[c], s4_ref, c, h)

    def toeplitz_step(slot, _):
        shift = b_tab[slot]
        unit = pk_ref[pl.ds(pl.multiple_of(slot * 16, 16), 16), :].astype(F32)
        unit = pltpu.roll(unit, shift, axis=1)
        zero_tile = jnp.zeros((8, W), F32)
        for c in range(3):
            rows = [
                jnp.broadcast_to(unit[3 * a + c : 3 * a + c + 1], (8, W)) for a in range(WL)
            ]
            strips = []
            for j in range(2):
                turned = [pltpu.roll(v, 8 * j, axis=1, stride=1, stride_axis=0) for v in rows]
                turned = [zero_tile] + turned + [zero_tile]
                keep = lane >= sub + (8 * j + shift)
                strips.append(
                    jnp.concatenate(
                        [jnp.where(keep, turned[a + 1], turned[a]) for a in range(KB)], axis=1
                    )
                )
            strip = jnp.concatenate(strips, axis=0).astype(BF16)
            toe_ref[slot, pl.ds(STEP * c, 16), :] = strip
            for j in range(16, STEP, 16):
                toe_ref[slot, pl.ds(STEP * c + j, 16), :] = pltpu.roll(strip, j, axis=1)
        return 0

    def slot_step(slot, _):
        row = row_tab[slot]
        shift = b_tab[slot]
        back = lax.rem(W - shift, W)
        frames = jnp.concatenate(
            [
                jnp.concatenate(
                    [x4_ref[c, pl.ds(row + H * a, MR), :] for a in range(KB)], axis=1
                )
                for c in range(3)
            ],
            axis=0,
        ).astype(BF16)
        corr = lax.dot_general(
            frames, toe_ref[slot], (((1,), (1,)), ((), ())), preferred_element_type=F32
        )
        terms = []
        for c in range(3):
            weight = mask_ref[c, st_tab[slot]].astype(F32)
            factor = pltpu.roll(s4_ref[c, pl.ds(row, MR), :], back, axis=1)
            mine = corr[MR * c : MR * (c + 1), STEP * c : STEP * (c + 1)]
            terms.append(mine * (factor[:, :STEP] * weight))
        acc_ref[slot] = terms[0] + terms[1] + terms[2]
        return 0

    def pass_on(c):
        for kind in range(1, X):
            record_copy(c, kind).wait_recv()
            record_copy(c, X - 1 + kind).start()

    prepare(g)
    pass_on(0)
    for k in range(1, S):
        packet_copy(k).wait_recv()
    lax.fori_loop(0, NS, toeplitz_step, 0, unroll=2)
    pass_on(1)
    pass_on(2)
    for c in range(3):
        record_copy(c, 0).wait_recv()
    prepare(mate)
    for k in range(1, X):
        prepare(lax.rem(xpos + X - k, X) * 2 + core)
    for k in range(1, X):
        for c in range(3):
            record_copy(c, X - 1 + k).wait_recv()
        prepare(lax.rem(xpos + X - k, X) * 2 + 1 - core)
    lax.fori_loop(0, NS, slot_step, 0, unroll=2)

    for group in range(NG):
        sums = []
        for t in range(group * TPG, (group + 1) * TPG):

            def add_pick(p, total):
                return total + acc_ref[tp_tab[t * S + p]]

            sums.append(lax.fori_loop(0, S, add_pick, jnp.zeros((MR, STEP), F32), unroll=8))
        side = jnp.concatenate(sums, axis=1)
        for d in range(S):
            part_ref[d, group // PK, pl.ds(group % PK * RD, RD), :] = side[RD * d : RD * (d + 1)]

    def sum_copy(k):
        target = lax.rem(me + k, S)
        return pltpu.make_async_remote_copy(
            src_ref=part_ref.at[target],
            dst_ref=land_ref.at[k - 1],
            send_sem=r_send.at[k - 1],
            recv_sem=r_recv.at[k - 1],
            device_id={"sta": target, "tpl": g},
            device_id_type=MESH,
        )

    for k in range(1, S):
        sum_copy(k).start()
    total = part_ref[me]
    for k in range(1, S):
        sum_copy(k).wait_recv()
        total = total + land_ref[k - 1]
    for t in range(G):
        m = t % TPG
        low = t // TPG % PK * RD
        for r in range(RD):
            out_ref[t : t + 1, STEP * r : STEP * (r + 1)] = total[
                t // TPG // PK, low + r : low + r + 1, STEP * m : STEP * (m + 1)
            ]

    for c in range(3):
        for kind in range(2 * X - 1):
            record_copy(c, kind).wait_send()
    for k in range(1, S):
        packet_copy(k).wait_send()
        sum_copy(k).wait_send()


def body(S, N, station_data, channel_mask, template_waves, pick_station, pick_lag):
    SL, samples = station_data.shape[1], station_data.shape[2]
    G, picks = pick_station.shape
    assert picks == S and template_waves.shape[1] == 1
    CAP = max(2, G // 8)
    RPS = samples // W
    RG = -(-(SL * RPS) // 8) * 8
    ND = NT // S
    STEP = 64 if ND % 64 == 0 else 16
    H = W // STEP
    MR = NT // STEP
    KB = -(-(L + 2 * STEP - 2) // W)
    PK = 8 // (ND // STEP)
    NP = -(-(G * STEP // W) // PK)
    X = N // 2
    NS = S * CAP
    dims = (S, N, SL, G, CAP, RPS, RG, ND, STEP)
    rows = N * RG * H
    vmem = pl.BlockSpec(memory_space=pltpu.VMEM)
    hbm = pl.BlockSpec(memory_space=pltpu.HBM)
    flops = 2 * NS * 3 * MR * STEP * KB * W
    result = pl.pallas_call(
        functools.partial(kernel, dims),
        out_shape=pltpu.VMEM((G, ND), F32),
        in_specs=[hbm] * 5,
        out_specs=vmem,
        scratch_shapes=[
            pltpu.VMEM(station_data.shape, F32),
            pltpu.VMEM((1, 3, G, L), BF16),
            pltpu.SMEM(channel_mask.shape, jnp.int32),
            pltpu.SMEM(pick_station.shape, jnp.int32),
            pltpu.SMEM(pick_lag.shape, jnp.int32),
            pltpu.VMEM((N, RG + 8, W), F32),
            pltpu.VMEM((N, RG + 8, W), F32),
            pltpu.VMEM((N, RG + 8, W), F32),
            pltpu.VMEM((6 * (RG + 8), W), F32),
            pltpu.VMEM((6 * (RG + 8), W), F32),
            pltpu.VMEM((6 * (RG + 8), W), F32),
            pltpu.VMEM((3, RG + 8, W), F32),
            pltpu.VMEM((3, rows, W), F32),
            pltpu.VMEM((3, rows, W), F32),
            pltpu.VMEM((G, 16, W), F32),
            pltpu.VMEM((NS * 16, W), BF16),
            pltpu.VMEM((NS * 16, W), BF16),
            pltpu.VMEM((NS, 3 * STEP, KB * W), BF16),
            pltpu.VMEM((NS + 1, MR, STEP), F32),
            pltpu.VMEM((S, NP, 8, W), F32),
            pltpu.VMEM((S - 1, NP, 8, W), F32),
            pltpu.SMEM((NS,), jnp.int32),
            pltpu.SMEM((NS,), jnp.int32),
            pltpu.SMEM((NS,), jnp.int32),
            pltpu.SMEM((G * S,), jnp.int32),
            pltpu.SemaphoreType.DMA((5,)),
            pltpu.SemaphoreType.DMA((3, 2 * X - 1)),
            pltpu.SemaphoreType.DMA((3, 2 * X - 1)),
            pltpu.SemaphoreType.DMA((S - 1,)),
            pltpu.SemaphoreType.DMA((S - 1,)),
            pltpu.SemaphoreType.DMA((S - 1,)),
            pltpu.SemaphoreType.DMA((S - 1,)),
        ],
        compiler_params=pltpu.CompilerParams(
            collective_id=0, has_side_effects=True, vmem_limit_bytes=63 * 1024 * 1024
        ),
        cost_estimate=pl.CostEstimate(flops=flops, bytes_accessed=1 << 20, transcendentals=0),
    )(station_data, jnp.transpose(template_waves, (1, 2, 0, 3)), channel_mask, pick_station, pick_lag)
    return result.T


def solution(mesh):
    in_specs = (
        P(None, ("sta", "tpl"), None),
        P(None, "sta"),
        P("tpl", "sta", None, None),
        P("tpl", None),
        P("tpl", None),
    )
    out_specs = P("sta", "tpl")
    run = functools.partial(body, mesh.shape["sta"], mesh.shape["tpl"])
    return jax.shard_map(run, mesh=mesh, in_specs=in_specs, out_specs=out_specs, check_vma=False)
```

```python
import functools

import jax
import jax.numpy as jnp
from jax import lax
from jax.experimental import pallas as pl
from jax.experimental.pallas import tpu as pltpu
from jax.sharding import PartitionSpec as P

NT = 1536
L = 640
LAGS = 1024
W = 128
EPS = 1e-05
MESH = pl.DeviceIdType.MESH
F32 = jnp.float32
BF16 = jnp.bfloat16

WL = L // W


def kernel(
    dims,
    data_hbm,
    waves_hbm,
    mask_hbm,
    ps_hbm,
    pl_hbm,
    out_ref,
    data_ref,
    waves_ref,
    mask_ref,
    ps_ref,
    pl_ref,
    buf0,
    buf1,
    buf2,
    d1_ref,
    d2_ref,
    tot_ref,
    sc_ref,
    x4_ref,
    s4_ref,
    uw_ref,
    pkt_ref,
    pk_ref,
    toe_ref,
    acc_ref,
    part_ref,
    land_ref,
    row_tab,
    b_tab,
    st_tab,
    tp_tab,
    l_sem,
    d_send,
    d_recv,
    p_send,
    p_recv,
    r_send,
    r_recv,
):
    S, N, SL, G, CAP, RPS, RG, ND, STEP = dims
    X = N // 2
    NS = S * CAP
    H = W // STEP
    MR = NT // STEP
    KB = -(-(L + 2 * STEP - 2) // W)
    TPG = W // STEP
    NG = G // TPG
    RD = ND // STEP
    PK = 8 // RD
    bufs = (buf0, buf1, buf2)
    me = lax.axis_index("sta")
    g = lax.axis_index("tpl")
    core = lax.rem(g, 2)
    xpos = g // 2
    mate = g + 1 - 2 * core
    peers = [{"sta": me, "tpl": mate}]
    far = []
    for k in range(1, X):
        far.append(lax.rem(xpos + k, X) * 2 + core)
        peers.append({"sta": me, "tpl": far[-1]})
    for k in range(1, S):
        peers.append({"sta": lax.rem(me + k, S), "tpl": g})

    local = [
        pltpu.make_async_copy(source, target, l_sem.at[i])
        for i, (source, target) in enumerate(
            [
                (data_hbm, data_ref),
                (waves_hbm, waves_ref),
                (ps_hbm, ps_ref),
                (pl_hbm, pl_ref),
                (mask_hbm, mask_ref),
            ]
        )
    ]
    for copy in local:
        copy.start()

    barrier = pltpu.get_barrier_semaphore()
    for peer in peers:
        pl.semaphore_signal(barrier, inc=1, device_id=peer, device_id_type=MESH)

    local[0].wait()
    for c in range(3):
        bufs[c][g, pl.ds(RG - 8, 8), :] = jnp.zeros((8, W), F32)
        for h in range(N):
            bufs[c][h, pl.ds(RG, 8), :] = jnp.zeros((8, W), F32)
        sc_ref[c, pl.ds(RG, 8), :] = jnp.zeros((8, W), F32)
        for b in range(RPS):
            bufs[c][g, pl.ds(b, SL, stride=RPS), :] = data_ref[c, :, b * W : (b + 1) * W]
    acc_ref[NS] = jnp.zeros((MR, STEP), F32)

    def record_copy(c, kind):
        if kind == 0:
            source, target = g, mate
        elif kind < X:
            source, target = g, far[kind - 1]
        else:
            source, target = lax.rem(xpos + X - (kind - X + 1), X) * 2 + core, mate
        return pltpu.make_async_remote_copy(
            src_ref=bufs[c].at[source, pl.ds(0, RG)],
            dst_ref=bufs[c].at[source, pl.ds(0, RG)],
            send_sem=d_send.at[c, kind],
            recv_sem=d_recv.at[c, kind],
            device_id={"sta": me, "tpl": target},
            device_id_type=MESH,
        )

    pl.semaphore_wait(barrier, len(peers))
    for c in range(3):
        for kind in list(range(1, X)) + [0]:
            record_copy(c, kind).start()

    local[1].wait()
    for c in range(3):
        values = waves_ref[0, c].astype(F32)
        centred = values - jnp.mean(values, axis=-1, keepdims=True)
        spread = jnp.sqrt(jnp.mean(centred * centred, axis=-1, keepdims=True) + EPS)
        unit = centred / spread
        for a in range(WL):
            uw_ref[:, 3 * a + c, :] = unit[:, a * W : (a + 1) * W]

    for copy in local[2:]:
        copy.wait()

    def packet_step(d, _):
        count = jnp.int32(0)
        chosen = [jnp.int32(0)] * CAP
        low = d * SL * N
        for t in range(G):
            station = ps_ref[t, me]
            mine = jnp.logical_and(station >= low, station < low + SL * N).astype(jnp.int32)
            for j in range(CAP):
                chosen[j] = jnp.where(mine * (count + 1) == j + 1, t, chosen[j])
            count = count + mine
        for j in range(CAP):
            row = pl.multiple_of((d * CAP + j) * 16, 16)
            pkt_ref[pl.ds(row, 16), :] = uw_ref[chosen[j]].astype(BF16)
        return 0

    lax.fori_loop(0, S, packet_step, 0)

    def packet_copy(k):
        target = lax.rem(me + k, S)
        return pltpu.make_async_remote_copy(
            src_ref=pkt_ref.at[pl.ds(pl.multiple_of(target * CAP * 16, 16), CAP * 16)],
            dst_ref=pk_ref.at[pl.ds(pl.multiple_of(me * CAP * 16, 16), CAP * 16)],
            send_sem=p_send.at[k - 1],
            recv_sem=p_recv.at[k - 1],
            device_id={"sta": target, "tpl": g},
            device_id_type=MESH,
        )

    for k in range(1, S):
        packet_copy(k).start()
    own_packet = pl.ds(pl.multiple_of(me * CAP * 16, 16), CAP * 16)
    pk_ref[own_packet, :] = pkt_ref[own_packet, :]

    def table_step(p, _):
        count = jnp.int32(0)
        stations = [jnp.int32(0)] * CAP
        lags = [jnp.int32(0)] * CAP
        low = me * SL * N
        for t in range(G):
            station = ps_ref[t, p]
            lag = pl_ref[t, p]
            mine = jnp.logical_and(station >= low, station < low + SL * N).astype(jnp.int32)
            tp_tab[t * S + p] = jnp.where(mine == 1, p * CAP + jnp.minimum(count, CAP - 1), NS)
            for j in range(CAP):
                here = mine * (count + 1) == j + 1
                stations[j] = jnp.where(here, station - low, stations[j])
                lags[j] = jnp.where(here, lag, lags[j])
            count = count + mine
        for j in range(CAP):
            holder = stations[j] // SL
            first = holder * RG + (stations[j] - holder * SL) * RPS
            row_tab[p * CAP + j] = first * H + lags[j] // STEP
            b_tab[p * CAP + j] = lax.rem(lags[j], STEP)
            st_tab[p * CAP + j] = stations[j]
        return 0

    lax.fori_loop(0, S, table_step, 0)

    lane = lax.broadcasted_iota(jnp.int32, (8, W), 1)
    sub = lax.broadcasted_iota(jnp.int32, (8, W), 0)
    ones_k = lax.broadcasted_iota(jnp.int32, (W, 2 * W), 0)
    ones_r = lax.broadcasted_iota(jnp.int32, (W, 2 * W), 1)
    window = jnp.logical_and(ones_k >= ones_r, ones_r < W)
    window = jnp.logical_or(window, ones_k < ones_r - W).astype(F32).astype(BF16)
    window = jnp.concatenate([window] * 3, axis=0)

    def edge_sums(values):
        high = values.astype(BF16)
        rest = values - high.astype(F32)
        middle = rest.astype(BF16)
        low = (rest - middle.astype(F32)).astype(BF16)
        parts = jnp.concatenate([low, middle, high], axis=1)
        return jnp.dot(parts, window, preferred_element_type=F32)

    def shifted_rows(source, target, c, h):
        wide = lax.broadcasted_iota(jnp.int32, (RG, W), 1)
        now = source[pl.ds(0, RG), :]
        after = source[pl.ds(1, RG), :]
        row = h * (RG * H)
        target[c, pl.ds(row, RG, stride=H), :] = now
        for q in range(1, H):
            target[c, pl.ds(row + q, RG, stride=H), :] = jnp.where(
                wide < W - STEP * q,
                pltpu.roll(now, W - STEP * q, axis=1),
                pltpu.roll(after, W - STEP * q, axis=1),
            )

    def prepare(h):
        for c in range(3):
            shifted_rows(bufs[c].at[h], x4_ref, c, h)
        x = jnp.concatenate([bufs[c][h] for c in range(3)], axis=0)
        edges = edge_sums(jnp.concatenate([x, x * x], axis=0))
        RE = RG + 8
        d1_ref[...] = edges[:, :W]
        d2_ref[...] = edges[:, W:]
        tot_ref[...] = edges[:, :W] + edges[:, W:]
        for c in range(3):
            means = []
            for q in range(2):
                at = (q * 3 + c) * RE
                total = d1_ref[pl.ds(at, RG), :] + d2_ref[pl.ds(at + WL, RG), :]
                for a in range(1, WL):
                    total += tot_ref[pl.ds(at + a, RG), :]
                means.append(total * (1.0 / L))
            one, two = means
            sc_ref[c, pl.ds(0, RG), :] = lax.rsqrt(two - one * one + EPS) * (1.0 / L)
            shifted_rows(sc_ref.at[c], s4_ref, c, h)

    def toeplitz_step(slot, _):
        shift = b_tab[slot]
        unit = pk_ref[pl.ds(pl.multiple_of(slot * 16, 16), 16), :].astype(F32)
        unit = pltpu.roll(unit, shift, axis=1)
        zero_tile = jnp.zeros((8, W), F32)
        for c in range(3):
            rows = [
                jnp.broadcast_to(unit[3 * a + c : 3 * a + c + 1], (8, W)) for a in range(WL)
            ]
            strips = []
            for j in range(2):
                turned = [pltpu.roll(v, 8 * j, axis=1, stride=1, stride_axis=0) for v in rows]
                turned = [zero_tile] + turned + [zero_tile]
                keep = lane >= sub + (8 * j + shift)
                strips.append(
                    jnp.concatenate(
                        [jnp.where(keep, turned[a + 1], turned[a]) for a in range(KB)], axis=1
                    )
                )
            strip = jnp.concatenate(strips, axis=0).astype(BF16)
            toe_ref[slot, pl.ds(STEP * c, 16), :] = strip
            for j in range(16, STEP, 16):
                toe_ref[slot, pl.ds(STEP * c + j, 16), :] = pltpu.roll(strip, j, axis=1)
        return 0

    def slot_step(slot, _):
        row = row_tab[slot]
        shift = b_tab[slot]
        back = lax.rem(W - shift, W)
        frames = jnp.concatenate(
            [
                jnp.concatenate(
                    [x4_ref[c, pl.ds(row + H * a, MR), :] for a in range(KB)], axis=1
                )
                for c in range(3)
            ],
            axis=0,
        ).astype(BF16)
        corr = lax.dot_general(
            frames, toe_ref[slot], (((1,), (1,)), ((), ())), preferred_element_type=F32
        )
        terms = []
        for c in range(3):
            weight = mask_ref[c, st_tab[slot]].astype(F32)
            factor = pltpu.roll(s4_ref[c, pl.ds(row, MR), :], back, axis=1)
            mine = corr[MR * c : MR * (c + 1), STEP * c : STEP * (c + 1)]
            terms.append(mine * (factor[:, :STEP] * weight))
        acc_ref[slot] = terms[0] + terms[1] + terms[2]
        return 0

    def pass_on(c):
        for kind in range(1, X):
            record_copy(c, kind).wait_recv()
            record_copy(c, X - 1 + kind).start()

    straight = NS if NS <= 16 else 2
    prepare(g)
    pass_on(0)
    for c in range(3):
        record_copy(c, 0).wait_recv()
    prepare(mate)
    pass_on(1)
    for k in range(1, S):
        packet_copy(k).wait_recv()
    lax.fori_loop(0, NS, toeplitz_step, 0, unroll=straight)
    pass_on(2)
    for k in range(1, X):
        prepare(lax.rem(xpos + X - k, X) * 2 + core)
    for k in range(1, X):
        for c in range(3):
            record_copy(c, X - 1 + k).wait_recv()
        prepare(lax.rem(xpos + X - k, X) * 2 + 1 - core)
    lax.fori_loop(0, NS, slot_step, 0, unroll=straight)

    for group in range(NG):
        sums = []
        for t in range(group * TPG, (group + 1) * TPG):

            def add_pick(p, total):
                return total + acc_ref[tp_tab[t * S + p]]

            sums.append(lax.fori_loop(0, S, add_pick, jnp.zeros((MR, STEP), F32), unroll=8))
        side = jnp.concatenate(sums, axis=1)
        for d in range(S):
            part_ref[d, group // PK, pl.ds(group % PK * RD, RD), :] = side[RD * d : RD * (d + 1)]

    def sum_copy(k):
        target = lax.rem(me + k, S)
        return pltpu.make_async_remote_copy(
            src_ref=part_ref.at[target],
            dst_ref=land_ref.at[k - 1],
            send_sem=r_send.at[k - 1],
            recv_sem=r_recv.at[k - 1],
            device_id={"sta": target, "tpl": g},
            device_id_type=MESH,
        )

    for k in range(1, S):
        sum_copy(k).start()
    total = part_ref[me]
    for k in range(1, S):
        sum_copy(k).wait_recv()
        total = total + land_ref[k - 1]
    for t in range(G):
        m = t % TPG
        low = t // TPG % PK * RD
        for r in range(RD):
            out_ref[t : t + 1, STEP * r : STEP * (r + 1)] = total[
                t // TPG // PK, low + r : low + r + 1, STEP * m : STEP * (m + 1)
            ]

    for c in range(3):
        for kind in range(2 * X - 1):
            record_copy(c, kind).wait_send()
    for k in range(1, S):
        packet_copy(k).wait_send()
        sum_copy(k).wait_send()


def body(S, N, station_data, channel_mask, template_waves, pick_station, pick_lag):
    SL, samples = station_data.shape[1], station_data.shape[2]
    G, picks = pick_station.shape
    assert picks == S and template_waves.shape[1] == 1
    CAP = max(2, G // 8)
    RPS = samples // W
    RG = -(-(SL * RPS) // 8) * 8
    ND = NT // S
    STEP = 64 if ND % 64 == 0 else 16
    H = W // STEP
    MR = NT // STEP
    KB = -(-(L + 2 * STEP - 2) // W)
    PK = 8 // (ND // STEP)
    NP = -(-(G * STEP // W) // PK)
    X = N // 2
    NS = S * CAP
    dims = (S, N, SL, G, CAP, RPS, RG, ND, STEP)
    rows = N * RG * H
    vmem = pl.BlockSpec(memory_space=pltpu.VMEM)
    hbm = pl.BlockSpec(memory_space=pltpu.HBM)
    flops = 2 * NS * 3 * MR * STEP * KB * W
    result = pl.pallas_call(
        functools.partial(kernel, dims),
        out_shape=pltpu.VMEM((G, ND), F32),
        in_specs=[hbm] * 5,
        out_specs=vmem,
        scratch_shapes=[
            pltpu.VMEM(station_data.shape, F32),
            pltpu.VMEM((1, 3, G, L), BF16),
            pltpu.SMEM(channel_mask.shape, jnp.int32),
            pltpu.SMEM(pick_station.shape, jnp.int32),
            pltpu.SMEM(pick_lag.shape, jnp.int32),
            pltpu.VMEM((N, RG + 8, W), F32),
            pltpu.VMEM((N, RG + 8, W), F32),
            pltpu.VMEM((N, RG + 8, W), F32),
            pltpu.VMEM((6 * (RG + 8), W), F32),
            pltpu.VMEM((6 * (RG + 8), W), F32),
            pltpu.VMEM((6 * (RG + 8), W), F32),
            pltpu.VMEM((3, RG + 8, W), F32),
            pltpu.VMEM((3, rows, W), F32),
            pltpu.VMEM((3, rows, W), F32),
            pltpu.VMEM((G, 16, W), F32),
            pltpu.VMEM((NS * 16, W), BF16),
            pltpu.VMEM((NS * 16, W), BF16),
            pltpu.VMEM((NS, 3 * STEP, KB * W), BF16),
            pltpu.VMEM((NS + 1, MR, STEP), F32),
            pltpu.VMEM((S, NP, 8, W), F32),
            pltpu.VMEM((S - 1, NP, 8, W), F32),
            pltpu.SMEM((NS,), jnp.int32),
            pltpu.SMEM((NS,), jnp.int32),
            pltpu.SMEM((NS,), jnp.int32),
            pltpu.SMEM((G * S,), jnp.int32),
            pltpu.SemaphoreType.DMA((5,)),
            pltpu.SemaphoreType.DMA((3, 2 * X - 1)),
            pltpu.SemaphoreType.DMA((3, 2 * X - 1)),
            pltpu.SemaphoreType.DMA((S - 1,)),
            pltpu.SemaphoreType.DMA((S - 1,)),
            pltpu.SemaphoreType.DMA((S - 1,)),
            pltpu.SemaphoreType.DMA((S - 1,)),
        ],
        compiler_params=pltpu.CompilerParams(
            collective_id=0, has_side_effects=True, vmem_limit_bytes=63 * 1024 * 1024
        ),
        cost_estimate=pl.CostEstimate(flops=flops, bytes_accessed=1 << 20, transcendentals=0),
    )(station_data, jnp.transpose(template_waves, (1, 2, 0, 3)), channel_mask, pick_station, pick_lag)
    return result.T


def solution(mesh):
    in_specs = (
        P(None, ("sta", "tpl"), None),
        P(None, "sta"),
        P("tpl", "sta", None, None),
        P("tpl", None),
        P("tpl", None),
    )
    out_specs = P("sta", "tpl")
    run = functools.partial(body, mesh.shape["sta"], mesh.shape["tpl"])
    return jax.shard_map(run, mesh=mesh, in_specs=in_specs, out_specs=out_specs, check_vma=False)
```

```python
import functools

import jax
import jax.numpy as jnp
from jax import lax
from jax.experimental import pallas as pl
from jax.experimental.pallas import tpu as pltpu
from jax.sharding import PartitionSpec as P

NT = 1536
L = 640
LAGS = 1024
W = 128
EPS = 1e-05
MESH = pl.DeviceIdType.MESH
F32 = jnp.float32
BF16 = jnp.bfloat16

WL = L // W


def kernel(
    dims,
    data_hbm,
    waves_hbm,
    mask_hbm,
    ps_hbm,
    pl_hbm,
    out_ref,
    data_ref,
    waves_ref,
    mask_ref,
    ps_ref,
    pl_ref,
    buf0,
    buf1,
    buf2,
    d1_ref,
    d2_ref,
    tot_ref,
    sc_ref,
    x4_ref,
    s4_ref,
    uw_ref,
    pkt_ref,
    pk_ref,
    toe_ref,
    acc_ref,
    part_ref,
    land_ref,
    row_tab,
    b_tab,
    st_tab,
    tp_tab,
    l_sem,
    d_send,
    d_recv,
    p_send,
    p_recv,
    r_send,
    r_recv,
):
    S, N, SL, G, CAP, RPS, RG, ND, STEP = dims
    X = N // 2
    NS = S * CAP
    H = W // STEP
    MR = NT // STEP
    KB = -(-(L + 2 * STEP - 2) // W)
    TPG = W // STEP
    NG = G // TPG
    RD = ND // STEP
    PK = 8 // RD
    bufs = (buf0, buf1, buf2)
    me = lax.axis_index("sta")
    g = lax.axis_index("tpl")
    core = lax.rem(g, 2)
    xpos = g // 2
    mate = g + 1 - 2 * core
    peers = [{"sta": me, "tpl": mate}]
    far = []
    for k in range(1, X):
        far.append(lax.rem(xpos + k, X) * 2 + core)
        peers.append({"sta": me, "tpl": far[-1]})
    for k in range(1, S):
        peers.append({"sta": lax.rem(me + k, S), "tpl": g})

    local = [
        pltpu.make_async_copy(source, target, l_sem.at[i])
        for i, (source, target) in enumerate(
            [
                (data_hbm, data_ref),
                (waves_hbm, waves_ref),
                (ps_hbm, ps_ref),
                (pl_hbm, pl_ref),
                (mask_hbm, mask_ref),
            ]
        )
    ]
    for copy in local:
        copy.start()

    barrier = pltpu.get_barrier_semaphore()
    for peer in peers:
        pl.semaphore_signal(barrier, inc=1, device_id=peer, device_id_type=MESH)

    local[0].wait()
    for c in range(3):
        bufs[c][g, pl.ds(RG - 8, 8), :] = jnp.zeros((8, W), F32)
        for h in range(N):
            bufs[c][h, pl.ds(RG, 8), :] = jnp.zeros((8, W), F32)
        sc_ref[c, pl.ds(RG, 8), :] = jnp.zeros((8, W), F32)
        for b in range(RPS):
            bufs[c][g, pl.ds(b, SL, stride=RPS), :] = data_ref[c, :, b * W : (b + 1) * W]
    acc_ref[NS] = jnp.zeros((MR, STEP), F32)

    def record_copy(c, kind):
        if kind == 0:
            source, target = g, mate
        elif kind < X:
            source, target = g, far[kind - 1]
        else:
            source, target = lax.rem(xpos + X - (kind - X + 1), X) * 2 + core, mate
        return pltpu.make_async_remote_copy(
            src_ref=bufs[c].at[source, pl.ds(0, RG)],
            dst_ref=bufs[c].at[source, pl.ds(0, RG)],
            send_sem=d_send.at[c, kind],
            recv_sem=d_recv.at[c, kind],
            device_id={"sta": me, "tpl": target},
            device_id_type=MESH,
        )

    pl.semaphore_wait(barrier, len(peers))
    for c in range(3):
        for kind in list(range(1, X)) + [0]:
            record_copy(c, kind).start()

    local[1].wait()
    for c in range(3):
        values = waves_ref[0, c].astype(F32)
        centred = values - jnp.mean(values, axis=-1, keepdims=True)
        spread = jnp.sqrt(jnp.mean(centred * centred, axis=-1, keepdims=True) + EPS)
        unit = centred / spread
        for a in range(WL):
            uw_ref[:, 3 * a + c, :] = unit[:, a * W : (a + 1) * W]

    for copy in local[2:]:
        copy.wait()

    def packet_step(d, _):
        count = jnp.int32(0)
        chosen = [jnp.int32(0)] * CAP
        low = d * SL * N
        for t in range(G):
            station = ps_ref[t, me]
            mine = jnp.logical_and(station >= low, station < low + SL * N).astype(jnp.int32)
            for j in range(CAP):
                chosen[j] = jnp.where(mine * (count + 1) == j + 1, t, chosen[j])
            count = count + mine
        for j in range(CAP):
            row = pl.multiple_of((d * CAP + j) * 16, 16)
            pkt_ref[pl.ds(row, 16), :] = uw_ref[chosen[j]].astype(BF16)
        return 0

    lax.fori_loop(0, S, packet_step, 0)

    def packet_copy(k):
        target = lax.rem(me + k, S)
        return pltpu.make_async_remote_copy(
            src_ref=pkt_ref.at[pl.ds(pl.multiple_of(target * CAP * 16, 16), CAP * 16)],
            dst_ref=pk_ref.at[pl.ds(pl.multiple_of(me * CAP * 16, 16), CAP * 16)],
            send_sem=p_send.at[k - 1],
            recv_sem=p_recv.at[k - 1],
            device_id={"sta": target, "tpl": g},
            device_id_type=MESH,
        )

    for k in range(1, S):
        packet_copy(k).start()
    own_packet = pl.ds(pl.multiple_of(me * CAP * 16, 16), CAP * 16)
    pk_ref[own_packet, :] = pkt_ref[own_packet, :]

    def table_step(p, _):
        count = jnp.int32(0)
        stations = [jnp.int32(0)] * CAP
        lags = [jnp.int32(0)] * CAP
        low = me * SL * N
        for t in range(G):
            station = ps_ref[t, p]
            lag = pl_ref[t, p]
            mine = jnp.logical_and(station >= low, station < low + SL * N).astype(jnp.int32)
            tp_tab[t * S + p] = jnp.where(mine == 1, p * CAP + jnp.minimum(count, CAP - 1), NS)
            for j in range(CAP):
                here = mine * (count + 1) == j + 1
                stations[j] = jnp.where(here, station - low, stations[j])
                lags[j] = jnp.where(here, lag, lags[j])
            count = count + mine
        for j in range(CAP):
            holder = stations[j] // SL
            first = holder * RG + (stations[j] - holder * SL) * RPS
            row_tab[p * CAP + j] = first * H + lags[j] // STEP
            b_tab[p * CAP + j] = lax.rem(lags[j], STEP)
            st_tab[p * CAP + j] = stations[j]
        return 0

    lax.fori_loop(0, S, table_step, 0)

    lane = lax.broadcasted_iota(jnp.int32, (8, W), 1)
    sub = lax.broadcasted_iota(jnp.int32, (8, W), 0)
    ones_k = lax.broadcasted_iota(jnp.int32, (W, 2 * W), 0)
    ones_r = lax.broadcasted_iota(jnp.int32, (W, 2 * W), 1)
    window = jnp.logical_and(ones_k >= ones_r, ones_r < W)
    window = jnp.logical_or(window, ones_k < ones_r - W).astype(F32).astype(BF16)
    window = jnp.concatenate([window] * 3, axis=0)

    def edge_sums(values):
        high = values.astype(BF16)
        rest = values - high.astype(F32)
        middle = rest.astype(BF16)
        low = (rest - middle.astype(F32)).astype(BF16)
        parts = jnp.concatenate([low, middle, high], axis=1)
        return jnp.dot(parts, window, preferred_element_type=F32)

    def shifted_rows(source, target, c, h):
        wide = lax.broadcasted_iota(jnp.int32, (RG, W), 1)
        now = source[pl.ds(0, RG), :]
        after = source[pl.ds(1, RG), :]
        row = h * (RG * H)
        target[c, pl.ds(row, RG, stride=H), :] = now
        for q in range(1, H):
            target[c, pl.ds(row + q, RG, stride=H), :] = jnp.where(
                wide < W - STEP * q,
                pltpu.roll(now, W - STEP * q, axis=1),
                pltpu.roll(after, W - STEP * q, axis=1),
            )

    def prepare(c, h):
        shifted_rows(bufs[c].at[h], x4_ref, c, h)
        x = bufs[c][h]
        edges = edge_sums(jnp.concatenate([x, x * x], axis=0))
        RE = RG + 8
        d1_ref[c] = edges[:, :W]
        d2_ref[c] = edges[:, W:]
        tot_ref[c] = edges[:, :W] + edges[:, W:]
        means = []
        for q in range(2):
            at = q * RE
            total = d1_ref[c, pl.ds(at, RG), :] + d2_ref[c, pl.ds(at + WL, RG), :]
            for a in range(1, WL):
                total += tot_ref[c, pl.ds(at + a, RG), :]
            means.append(total * (1.0 / L))
        one, two = means
        sc_ref[c, pl.ds(0, RG), :] = lax.rsqrt(two - one * one + EPS) * (1.0 / L)
        shifted_rows(sc_ref.at[c], s4_ref, c, h)

    def strips_of(c):
        def step(slot, _):
            shift = b_tab[slot]
            unit = pk_ref[pl.ds(pl.multiple_of(slot * 16, 16), 16), :].astype(F32)
            unit = pltpu.roll(unit, shift, axis=1)
            zero_tile = jnp.zeros((8, W), F32)
            rows = [
                jnp.broadcast_to(unit[3 * a + c : 3 * a + c + 1], (8, W)) for a in range(WL)
            ]
            for j in range(0, STEP // 8, 2):
                strips = []
                for i in (j, j + 1):
                    turned = [
                        pltpu.roll(v, 8 * i, axis=1, stride=1, stride_axis=0) for v in rows
                    ]
                    turned = [zero_tile] + turned + [zero_tile]
                    keep = lane >= sub + (8 * i + shift)
                    strips.append(
                        jnp.concatenate(
                            [jnp.where(keep, turned[a + 1], turned[a]) for a in range(KB)], axis=1
                        )
                    )
                toe_ref[slot * 3 + c, pl.ds(8 * j, 16), :] = jnp.concatenate(
                    strips, axis=0
                ).astype(BF16)
            return 0

        lax.fori_loop(0, NS, step, 0, unroll=4)

    def slots_of(c):
        def step(slot, _):
            row = row_tab[slot]
            shift = b_tab[slot]
            weight = mask_ref[c, st_tab[slot]].astype(F32)
            frames = jnp.concatenate(
                [x4_ref[c, pl.ds(row + H * a, MR), :] for a in range(KB)], axis=1
            ).astype(BF16)
            corr = lax.dot_general(
                frames, toe_ref[slot * 3 + c], (((1,), (1,)), ((), ())), preferred_element_type=F32
            )
            factor = pltpu.roll(s4_ref[c, pl.ds(row, MR), :], lax.rem(W - shift, W), axis=1)
            term = corr * (factor[:, :STEP] * weight)
            if c == 0:
                acc_ref[slot] = term
            else:
                acc_ref[slot] += term
            return 0

        lax.fori_loop(0, NS, step, 0, unroll=4)

    def pass_on(c):
        for kind in range(1, X):
            record_copy(c, kind).wait_recv()
            record_copy(c, X - 1 + kind).start()

    for c in range(3):
        prepare(c, g)
    for k in range(1, S):
        packet_copy(k).wait_recv()
    strips_of(0)
    pass_on(0)
    strips_of(1)
    pass_on(1)
    strips_of(2)
    for c in range(3):
        record_copy(c, 0).wait_recv()
        prepare(c, mate)
        for k in range(1, X):
            prepare(c, lax.rem(xpos + X - k, X) * 2 + core)
        if c == 1:
            pass_on(2)
        for k in range(1, X):
            record_copy(c, X - 1 + k).wait_recv()
            prepare(c, lax.rem(xpos + X - k, X) * 2 + 1 - core)
        slots_of(c)

    for group in range(NG):
        sums = []
        for t in range(group * TPG, (group + 1) * TPG):

            def add_pick(p, total):
                return total + acc_ref[tp_tab[t * S + p]]

            sums.append(lax.fori_loop(0, S, add_pick, jnp.zeros((MR, STEP), F32), unroll=8))
        side = jnp.concatenate(sums, axis=1)
        for d in range(S):
            part_ref[d, group // PK, pl.ds(group % PK * RD, RD), :] = side[RD * d : RD * (d + 1)]

    def sum_copy(k):
        target = lax.rem(me + k, S)
        return pltpu.make_async_remote_copy(
            src_ref=part_ref.at[target],
            dst_ref=land_ref.at[k - 1],
            send_sem=r_send.at[k - 1],
            recv_sem=r_recv.at[k - 1],
            device_id={"sta": target, "tpl": g},
            device_id_type=MESH,
        )

    for k in range(1, S):
        sum_copy(k).start()
    total = part_ref[me]
    for k in range(1, S):
        sum_copy(k).wait_recv()
        total = total + land_ref[k - 1]
    for t in range(G):
        m = t % TPG
        low = t // TPG % PK * RD
        for r in range(RD):
            out_ref[t : t + 1, STEP * r : STEP * (r + 1)] = total[
                t // TPG // PK, low + r : low + r + 1, STEP * m : STEP * (m + 1)
            ]

    for c in range(3):
        for kind in range(2 * X - 1):
            record_copy(c, kind).wait_send()
    for k in range(1, S):
        packet_copy(k).wait_send()
        sum_copy(k).wait_send()


def body(S, N, station_data, channel_mask, template_waves, pick_station, pick_lag):
    SL, samples = station_data.shape[1], station_data.shape[2]
    G, picks = pick_station.shape
    assert picks == S and template_waves.shape[1] == 1
    CAP = max(2, G // 8)
    RPS = samples // W
    RG = -(-(SL * RPS) // 8) * 8
    ND = NT // S
    STEP = 64 if ND % 64 == 0 else 16
    H = W // STEP
    MR = NT // STEP
    KB = -(-(L + 2 * STEP - 2) // W)
    PK = 8 // (ND // STEP)
    NP = -(-(G * STEP // W) // PK)
    X = N // 2
    NS = S * CAP
    dims = (S, N, SL, G, CAP, RPS, RG, ND, STEP)
    rows = N * RG * H
    vmem = pl.BlockSpec(memory_space=pltpu.VMEM)
    hbm = pl.BlockSpec(memory_space=pltpu.HBM)
    flops = 2 * NS * 3 * MR * STEP * KB * W
    result = pl.pallas_call(
        functools.partial(kernel, dims),
        out_shape=pltpu.VMEM((G, ND), F32),
        in_specs=[hbm] * 5,
        out_specs=vmem,
        scratch_shapes=[
            pltpu.VMEM(station_data.shape, F32),
            pltpu.VMEM((1, 3, G, L), BF16),
            pltpu.SMEM(channel_mask.shape, jnp.int32),
            pltpu.SMEM(pick_station.shape, jnp.int32),
            pltpu.SMEM(pick_lag.shape, jnp.int32),
            pltpu.VMEM((N, RG + 8, W), F32),
            pltpu.VMEM((N, RG + 8, W), F32),
            pltpu.VMEM((N, RG + 8, W), F32),
            pltpu.VMEM((3, 2 * (RG + 8), W), F32),
            pltpu.VMEM((3, 2 * (RG + 8), W), F32),
            pltpu.VMEM((3, 2 * (RG + 8), W), F32),
            pltpu.VMEM((3, RG + 8, W), F32),
            pltpu.VMEM((3, rows, W), F32),
            pltpu.VMEM((3, rows, W), F32),
            pltpu.VMEM((G, 16, W), F32),
            pltpu.VMEM((NS * 16, W), BF16),
            pltpu.VMEM((NS * 16, W), BF16),
            pltpu.VMEM((NS * 3, STEP, KB * W), BF16),
            pltpu.VMEM((NS + 1, MR, STEP), F32),
            pltpu.VMEM((S, NP, 8, W), F32),
            pltpu.VMEM((S - 1, NP, 8, W), F32),
            pltpu.SMEM((NS,), jnp.int32),
            pltpu.SMEM((NS,), jnp.int32),
            pltpu.SMEM((NS,), jnp.int32),
            pltpu.SMEM((G * S,), jnp.int32),
            pltpu.SemaphoreType.DMA((5,)),
            pltpu.SemaphoreType.DMA((3, 2 * X - 1)),
            pltpu.SemaphoreType.DMA((3, 2 * X - 1)),
            pltpu.SemaphoreType.DMA((S - 1,)),
            pltpu.SemaphoreType.DMA((S - 1,)),
            pltpu.SemaphoreType.DMA((S - 1,)),
            pltpu.SemaphoreType.DMA((S - 1,)),
        ],
        compiler_params=pltpu.CompilerParams(
            collective_id=0, has_side_effects=True, vmem_limit_bytes=63 * 1024 * 1024
        ),
        cost_estimate=pl.CostEstimate(flops=flops, bytes_accessed=1 << 20, transcendentals=0),
    )(station_data, jnp.transpose(template_waves, (1, 2, 0, 3)), channel_mask, pick_station, pick_lag)
    return result.T


def solution(mesh):
    in_specs = (
        P(None, ("sta", "tpl"), None),
        P(None, "sta"),
        P("tpl", "sta", None, None),
        P("tpl", None),
        P("tpl", None),
    )
    out_specs = P("sta", "tpl")
    run = functools.partial(body, mesh.shape["sta"], mesh.shape["tpl"])
    return jax.shard_map(run, mesh=mesh, in_specs=in_specs, out_specs=out_specs, check_vma=False)
```

```python
import functools

import jax
import jax.numpy as jnp
from jax import lax
from jax.experimental import pallas as pl
from jax.experimental.pallas import tpu as pltpu
from jax.sharding import PartitionSpec as P

NT = 1536
L = 640
LAGS = 1024
W = 128
EPS = 1e-05
MESH = pl.DeviceIdType.MESH
F32 = jnp.float32
BF16 = jnp.bfloat16

WL = L // W


def kernel(
    dims,
    data_hbm,
    waves_hbm,
    mask_hbm,
    ps_hbm,
    pl_hbm,
    out_ref,
    data_ref,
    waves_ref,
    mask_ref,
    ps_ref,
    pl_ref,
    buf0,
    buf1,
    buf2,
    d1_ref,
    d2_ref,
    tot_ref,
    sc_ref,
    x4_ref,
    s4_ref,
    uw_ref,
    pkt_ref,
    pk_ref,
    toe_ref,
    acc_ref,
    part_ref,
    land_ref,
    row_tab,
    b_tab,
    st_tab,
    tp_tab,
    l_sem,
    d_send,
    d_recv,
    p_send,
    p_recv,
    r_send,
    r_recv,
):
    S, N, SL, G, CAP, RPS, RG, ND, STEP = dims
    X = N // 2
    NS = S * CAP
    H = W // STEP
    MR = NT // STEP
    KB = -(-(L + 2 * STEP - 2) // W)
    TPG = W // STEP
    NG = G // TPG
    RD = ND // STEP
    PK = 8 // RD
    bufs = (buf0, buf1, buf2)
    me = lax.axis_index("sta")
    g = lax.axis_index("tpl")
    core = lax.rem(g, 2)
    xpos = g // 2
    mate = g + 1 - 2 * core
    peers = [{"sta": me, "tpl": mate}]
    far = []
    for k in range(1, X):
        far.append(lax.rem(xpos + k, X) * 2 + core)
        peers.append({"sta": me, "tpl": far[-1]})
    for k in range(1, S):
        peers.append({"sta": lax.rem(me + k, S), "tpl": g})

    local = [
        pltpu.make_async_copy(source, target, l_sem.at[i])
        for i, (source, target) in enumerate(
            [
                (data_hbm, data_ref),
                (waves_hbm, waves_ref),
                (ps_hbm, ps_ref),
                (pl_hbm, pl_ref),
                (mask_hbm, mask_ref),
            ]
        )
    ]
    for copy in local:
        copy.start()

    barrier = pltpu.get_barrier_semaphore()
    for peer in peers:
        pl.semaphore_signal(barrier, inc=1, device_id=peer, device_id_type=MESH)

    local[0].wait()
    for c in range(3):
        bufs[c][g, pl.ds(RG - 8, 8), :] = jnp.zeros((8, W), F32)
        for h in range(N):
            bufs[c][h, pl.ds(RG, 8), :] = jnp.zeros((8, W), F32)
        for m in range(2):
            sc_ref[m * 3 + c, pl.ds(RG, 8), :] = jnp.zeros((8, W), F32)
        for b in range(RPS):
            bufs[c][g, pl.ds(b, SL, stride=RPS), :] = data_ref[c, :, b * W : (b + 1) * W]
    acc_ref[NS] = jnp.zeros((MR, STEP), F32)

    def record_copy(c, kind):
        if kind == 0:
            source, target = g, mate
        elif kind < X:
            source, target = g, far[kind - 1]
        else:
            source, target = lax.rem(xpos + X - (kind - X + 1), X) * 2 + core, mate
        return pltpu.make_async_remote_copy(
            src_ref=bufs[c].at[source, pl.ds(0, RG)],
            dst_ref=bufs[c].at[source, pl.ds(0, RG)],
            send_sem=d_send.at[c, kind],
            recv_sem=d_recv.at[c, kind],
            device_id={"sta": me, "tpl": target},
            device_id_type=MESH,
        )

    pl.semaphore_wait(barrier, len(peers))
    for c in range(3):
        for kind in list(range(1, X)) + [0]:
            record_copy(c, kind).start()

    local[1].wait()
    for c in range(3):
        values = waves_ref[0, c].astype(F32)
        centred = values - jnp.mean(values, axis=-1, keepdims=True)
        spread = jnp.sqrt(jnp.mean(centred * centred, axis=-1, keepdims=True) + EPS)
        unit = centred / spread
        for a in range(WL):
            uw_ref[:, 3 * a + c, :] = unit[:, a * W : (a + 1) * W]

    for copy in local[2:]:
        copy.wait()

    def packet_step(d, _):
        count = jnp.int32(0)
        chosen = [jnp.int32(0)] * CAP
        low = d * SL * N
        for t in range(G):
            station = ps_ref[t, me]
            mine = jnp.logical_and(station >= low, station < low + SL * N).astype(jnp.int32)
            for j in range(CAP):
                chosen[j] = jnp.where(mine * (count + 1) == j + 1, t, chosen[j])
            count = count + mine
        for j in range(CAP):
            row = pl.multiple_of((d * CAP + j) * 16, 16)
            pkt_ref[pl.ds(row, 16), :] = uw_ref[chosen[j]].astype(BF16)
        return 0

    lax.fori_loop(0, S, packet_step, 0)

    def packet_copy(k):
        target = lax.rem(me + k, S)
        return pltpu.make_async_remote_copy(
            src_ref=pkt_ref.at[pl.ds(pl.multiple_of(target * CAP * 16, 16), CAP * 16)],
            dst_ref=pk_ref.at[pl.ds(pl.multiple_of(me * CAP * 16, 16), CAP * 16)],
            send_sem=p_send.at[k - 1],
            recv_sem=p_recv.at[k - 1],
            device_id={"sta": target, "tpl": g},
            device_id_type=MESH,
        )

    for k in range(1, S):
        packet_copy(k).start()
    own_packet = pl.ds(pl.multiple_of(me * CAP * 16, 16), CAP * 16)
    pk_ref[own_packet, :] = pkt_ref[own_packet, :]

    def table_step(p, _):
        count = jnp.int32(0)
        stations = [jnp.int32(0)] * CAP
        lags = [jnp.int32(0)] * CAP
        low = me * SL * N
        for t in range(G):
            station = ps_ref[t, p]
            lag = pl_ref[t, p]
            mine = jnp.logical_and(station >= low, station < low + SL * N).astype(jnp.int32)
            tp_tab[t * S + p] = jnp.where(mine == 1, p * CAP + jnp.minimum(count, CAP - 1), NS)
            for j in range(CAP):
                here = mine * (count + 1) == j + 1
                stations[j] = jnp.where(here, station - low, stations[j])
                lags[j] = jnp.where(here, lag, lags[j])
            count = count + mine
        for j in range(CAP):
            holder = stations[j] // SL
            first = holder * RG + (stations[j] - holder * SL) * RPS
            row_tab[p * CAP + j] = first * H + lags[j] // STEP
            b_tab[p * CAP + j] = lax.rem(lags[j], STEP)
            st_tab[p * CAP + j] = stations[j]
        return 0

    lax.fori_loop(0, S, table_step, 0)

    lane = lax.broadcasted_iota(jnp.int32, (8, W), 1)
    sub = lax.broadcasted_iota(jnp.int32, (8, W), 0)
    ones_k = lax.broadcasted_iota(jnp.int32, (W, 2 * W), 0)
    ones_r = lax.broadcasted_iota(jnp.int32, (W, 2 * W), 1)
    window = jnp.logical_and(ones_k >= ones_r, ones_r < W)
    window = jnp.logical_or(window, ones_k < ones_r - W).astype(F32).astype(BF16)
    window = jnp.concatenate([window] * 3, axis=0)

    def edge_sums(values):
        high = values.astype(BF16)
        rest = values - high.astype(F32)
        middle = rest.astype(BF16)
        low = (rest - middle.astype(F32)).astype(BF16)
        parts = jnp.concatenate([low, middle, high], axis=1)
        return jnp.dot(parts, window, preferred_element_type=F32)

    def shifted_rows(source, target, c, h):
        wide = lax.broadcasted_iota(jnp.int32, (RG, W), 1)
        now = source[pl.ds(0, RG), :]
        after = source[pl.ds(1, RG), :]
        row = h * (RG * H)
        target[c, pl.ds(row, RG, stride=H), :] = now
        for q in range(1, H):
            target[c, pl.ds(row + q, RG, stride=H), :] = jnp.where(
                wide < W - STEP * q,
                pltpu.roll(now, W - STEP * q, axis=1),
                pltpu.roll(after, W - STEP * q, axis=1),
            )

    def prepare(pair):
        RE = RG + 8
        held = [bufs[c][h] for h in pair for c in range(3)]
        for i, h in enumerate(pair):
            for c in range(3):
                shifted_rows(bufs[c].at[h], x4_ref, c, h)
        x = jnp.concatenate(held, axis=0)
        edges = edge_sums(jnp.concatenate([x, x * x], axis=0))
        d1_ref[...] = edges[:, :W]
        d2_ref[...] = edges[:, W:]
        tot_ref[...] = edges[:, :W] + edges[:, W:]
        for i, h in enumerate(pair):
            for c in range(3):
                means = []
                for q in range(2):
                    at = (q * 6 + i * 3 + c) * RE
                    total = d1_ref[pl.ds(at, RG), :] + d2_ref[pl.ds(at + WL, RG), :]
                    for a in range(1, WL):
                        total += tot_ref[pl.ds(at + a, RG), :]
                    means.append(total * (1.0 / L))
                one, two = means
                scale = lax.rsqrt(two - one * one + EPS) * (1.0 / L)
                sc_ref[i * 3 + c, pl.ds(0, RG), :] = scale
                shifted_rows(sc_ref.at[i * 3 + c], s4_ref, c, h)

    def toeplitz_step(slot, _):
        shift = b_tab[slot]
        unit = pk_ref[pl.ds(pl.multiple_of(slot * 16, 16), 16), :].astype(F32)
        unit = pltpu.roll(unit, shift, axis=1)
        zero_tile = jnp.zeros((8, W), F32)
        for c in range(3):
            rows = [
                jnp.broadcast_to(unit[3 * a + c : 3 * a + c + 1], (8, W)) for a in range(WL)
            ]
            strips = []
            for j in range(2):
                turned = [pltpu.roll(v, 8 * j, axis=1, stride=1, stride_axis=0) for v in rows]
                turned = [zero_tile] + turned + [zero_tile]
                keep = lane >= sub + (8 * j + shift)
                strips.append(
                    jnp.concatenate(
                        [jnp.where(keep, turned[a + 1], turned[a]) for a in range(KB)], axis=1
                    )
                )
            strip = jnp.concatenate(strips, axis=0).astype(BF16)
            toe_ref[slot, pl.ds(STEP * c, 16), :] = strip
            for j in range(16, STEP, 16):
                toe_ref[slot, pl.ds(STEP * c + j, 16), :] = pltpu.roll(strip, j, axis=1)
        return 0

    def slot_step(slot, _):
        row = row_tab[slot]
        shift = b_tab[slot]
        back = lax.rem(W - shift, W)
        frames = jnp.concatenate(
            [
                jnp.concatenate(
                    [x4_ref[c, pl.ds(row + H * a, MR), :] for a in range(KB)], axis=1
                )
                for c in range(3)
            ],
            axis=0,
        ).astype(BF16)
        corr = lax.dot_general(
            frames, toe_ref[slot], (((1,), (1,)), ((), ())), preferred_element_type=F32
        )
        terms = []
        for c in range(3):
            weight = mask_ref[c, st_tab[slot]].astype(F32)
            factor = pltpu.roll(s4_ref[c, pl.ds(row, MR), :], back, axis=1)
            mine = corr[MR * c : MR * (c + 1), STEP * c : STEP * (c + 1)]
            terms.append(mine * (factor[:, :STEP] * weight))
        acc_ref[slot] = terms[0] + terms[1] + terms[2]
        return 0

    def pass_on(c):
        for kind in range(1, X):
            record_copy(c, kind).wait_recv()
            record_copy(c, X - 1 + kind).start()

    for c in range(3):
        record_copy(c, 0).wait_recv()
    pass_on(0)
    for k in range(1, S):
        packet_copy(k).wait_recv()

    def two_strips(i, _):
        toeplitz_step(2 * i, 0)
        toeplitz_step(2 * i + 1, 0)
        return 0

    def pair_step(k, _):
        chip = lax.rem(xpos + X - k, X) * 2
        prepare((chip + core, chip + 1 - core))

        @pl.when(k == 0)
        def _():
            pass_on(1)
            pass_on(2)

        lax.fori_loop(k * (NS // X // 2), (k + 1) * (NS // X // 2), two_strips, 0)

        @pl.when(k == 0)
        def _():
            for kind in range(X, 2 * X - 1):
                for c in range(3):
                    record_copy(c, kind).wait_recv()

        return 0

    lax.fori_loop(0, X, pair_step, 0)
    lax.fori_loop(0, NS, slot_step, 0, unroll=2)

    for group in range(NG):
        sums = []
        for t in range(group * TPG, (group + 1) * TPG):

            def add_pick(p, total):
                return total + acc_ref[tp_tab[t * S + p]]

            sums.append(lax.fori_loop(0, S, add_pick, jnp.zeros((MR, STEP), F32), unroll=8))
        side = jnp.concatenate(sums, axis=1)
        for d in range(S):
            part_ref[d, group // PK, pl.ds(group % PK * RD, RD), :] = side[RD * d : RD * (d + 1)]

    def sum_copy(k):
        target = lax.rem(me + k, S)
        return pltpu.make_async_remote_copy(
            src_ref=part_ref.at[target],
            dst_ref=land_ref.at[k - 1],
            send_sem=r_send.at[k - 1],
            recv_sem=r_recv.at[k - 1],
            device_id={"sta": target, "tpl": g},
            device_id_type=MESH,
        )

    for k in range(1, S):
        sum_copy(k).start()
    total = part_ref[me]
    for k in range(1, S):
        sum_copy(k).wait_recv()
        total = total + land_ref[k - 1]
    for t in range(G):
        m = t % TPG
        low = t // TPG % PK * RD
        for r in range(RD):
            out_ref[t : t + 1, STEP * r : STEP * (r + 1)] = total[
                t // TPG // PK, low + r : low + r + 1, STEP * m : STEP * (m + 1)
            ]

    for c in range(3):
        for kind in range(2 * X - 1):
            record_copy(c, kind).wait_send()
    for k in range(1, S):
        packet_copy(k).wait_send()
        sum_copy(k).wait_send()


def body(S, N, station_data, channel_mask, template_waves, pick_station, pick_lag):
    SL, samples = station_data.shape[1], station_data.shape[2]
    G, picks = pick_station.shape
    assert N % 2 == 0 and picks == S and template_waves.shape[1] == 1
    CAP = max(2, G // 8)
    RPS = samples // W
    RG = -(-(SL * RPS) // 8) * 8
    ND = NT // S
    STEP = 64 if ND % 64 == 0 else 16
    H = W // STEP
    MR = NT // STEP
    KB = -(-(L + 2 * STEP - 2) // W)
    PK = 8 // (ND // STEP)
    NP = -(-(G * STEP // W) // PK)
    X = N // 2
    NS = S * CAP
    dims = (S, N, SL, G, CAP, RPS, RG, ND, STEP)
    rows = N * RG * H
    vmem = pl.BlockSpec(memory_space=pltpu.VMEM)
    hbm = pl.BlockSpec(memory_space=pltpu.HBM)
    flops = 2 * NS * 3 * MR * STEP * KB * W
    result = pl.pallas_call(
        functools.partial(kernel, dims),
        out_shape=pltpu.VMEM((G, ND), F32),
        in_specs=[hbm] * 5,
        out_specs=vmem,
        scratch_shapes=[
            pltpu.VMEM(station_data.shape, F32),
            pltpu.VMEM((1, 3, G, L), BF16),
            pltpu.SMEM(channel_mask.shape, jnp.int32),
            pltpu.SMEM(pick_station.shape, jnp.int32),
            pltpu.SMEM(pick_lag.shape, jnp.int32),
            pltpu.VMEM((N, RG + 8, W), F32),
            pltpu.VMEM((N, RG + 8, W), F32),
            pltpu.VMEM((N, RG + 8, W), F32),
            pltpu.VMEM((12 * (RG + 8), W), F32),
            pltpu.VMEM((12 * (RG + 8), W), F32),
            pltpu.VMEM((12 * (RG + 8), W), F32),
            pltpu.VMEM((6, RG + 8, W), F32),
            pltpu.VMEM((3, rows, W), F32),
            pltpu.VMEM((3, rows, W), F32),
            pltpu.VMEM((G, 16, W), F32),
            pltpu.VMEM((NS * 16, W), BF16),
            pltpu.VMEM((NS * 16, W), BF16),
            pltpu.VMEM((NS, 3 * STEP, KB * W), BF16),
            pltpu.VMEM((NS + 1, MR, STEP), F32),
            pltpu.VMEM((S, NP, 8, W), F32),
            pltpu.VMEM((S - 1, NP, 8, W), F32),
            pltpu.SMEM((NS,), jnp.int32),
            pltpu.SMEM((NS,), jnp.int32),
            pltpu.SMEM((NS,), jnp.int32),
            pltpu.SMEM((G * S,), jnp.int32),
            pltpu.SemaphoreType.DMA((5,)),
            pltpu.SemaphoreType.DMA((3, 2 * X - 1)),
            pltpu.SemaphoreType.DMA((3, 2 * X - 1)),
            pltpu.SemaphoreType.DMA((S - 1,)),
            pltpu.SemaphoreType.DMA((S - 1,)),
            pltpu.SemaphoreType.DMA((S - 1,)),
            pltpu.SemaphoreType.DMA((S - 1,)),
        ],
        compiler_params=pltpu.CompilerParams(
            collective_id=0, has_side_effects=True, vmem_limit_bytes=63 * 1024 * 1024
        ),
        cost_estimate=pl.CostEstimate(flops=flops, bytes_accessed=1 << 20, transcendentals=0),
    )(station_data, jnp.transpose(template_waves, (1, 2, 0, 3)), channel_mask, pick_station, pick_lag)
    return result.T


def solution(mesh):
    in_specs = (
        P(None, ("sta", "tpl"), None),
        P(None, "sta"),
        P("tpl", "sta", None, None),
        P("tpl", None),
        P("tpl", None),
    )
    out_specs = P("sta", "tpl")
    run = functools.partial(body, mesh.shape["sta"], mesh.shape["tpl"])
    return jax.shard_map(run, mesh=mesh, in_specs=in_specs, out_specs=out_specs, check_vma=False)
```

```python
import functools

import jax
import jax.numpy as jnp
from jax import lax
from jax.experimental import pallas as pl
from jax.experimental.pallas import tpu as pltpu
from jax.sharding import PartitionSpec as P

NT = 1536
L = 640
LAGS = 1024
W = 128
EPS = 1e-05
MESH = pl.DeviceIdType.MESH
F32 = jnp.float32
BF16 = jnp.bfloat16

WL = L // W


def kernel(
    dims,
    data_hbm,
    waves_hbm,
    mask_hbm,
    ps_hbm,
    pl_hbm,
    out_ref,
    data_ref,
    waves_ref,
    mask_ref,
    ps_ref,
    pl_ref,
    buf0,
    buf1,
    buf2,
    d1_ref,
    d2_ref,
    tot_ref,
    sc_ref,
    x4_ref,
    s4_ref,
    uw_ref,
    pkt_ref,
    pk_ref,
    toe_ref,
    acc_ref,
    part_ref,
    land_ref,
    row_tab,
    b_tab,
    st_tab,
    tp_tab,
    l_sem,
    d_send,
    d_recv,
    p_send,
    p_recv,
    r_send,
    r_recv,
):
    S, N, SL, G, CAP, RPS, RG, ND, STEP = dims
    X = N // 2
    NS = S * CAP
    H = W // STEP
    MR = NT // STEP
    KB = -(-(L + 2 * STEP - 2) // W)
    TPG = W // STEP
    NG = G // TPG
    RD = ND // STEP
    PK = 8 // RD
    bufs = (buf0, buf1, buf2)
    me = lax.axis_index("sta")
    g = lax.axis_index("tpl")
    core = lax.rem(g, 2)
    xpos = g // 2
    mate = g + 1 - 2 * core
    peers = [{"sta": me, "tpl": mate}]
    far = []
    for k in range(1, X):
        far.append(lax.rem(xpos + k, X) * 2 + core)
        peers.append({"sta": me, "tpl": far[-1]})
    for k in range(1, S):
        peers.append({"sta": lax.rem(me + k, S), "tpl": g})

    local = [
        pltpu.make_async_copy(source, target, l_sem.at[i])
        for i, (source, target) in enumerate(
            [
                (data_hbm, data_ref),
                (waves_hbm, waves_ref),
                (ps_hbm, ps_ref),
                (pl_hbm, pl_ref),
                (mask_hbm, mask_ref),
            ]
        )
    ]
    for copy in local:
        copy.start()

    barrier = pltpu.get_barrier_semaphore()
    for peer in peers:
        pl.semaphore_signal(barrier, inc=1, device_id=peer, device_id_type=MESH)

    local[0].wait()
    for c in range(3):
        bufs[c][g, pl.ds(RG - 8, 8), :] = jnp.zeros((8, W), F32)
        for h in range(N):
            bufs[c][h, pl.ds(RG, 8), :] = jnp.zeros((8, W), F32)
        for m in range(2):
            sc_ref[m * 3 + c, pl.ds(RG, 8), :] = jnp.zeros((8, W), F32)
        for b in range(RPS):
            bufs[c][g, pl.ds(b, SL, stride=RPS), :] = data_ref[c, :, b * W : (b + 1) * W]
    acc_ref[NS] = jnp.zeros((MR, STEP), F32)

    def record_copy(c, kind):
        if kind == 0:
            source, target = g, mate
        elif kind < X:
            source, target = g, far[kind - 1]
        else:
            source, target = lax.rem(xpos + X - (kind - X + 1), X) * 2 + core, mate
        return pltpu.make_async_remote_copy(
            src_ref=bufs[c].at[source, pl.ds(0, RG)],
            dst_ref=bufs[c].at[source, pl.ds(0, RG)],
            send_sem=d_send.at[c, kind],
            recv_sem=d_recv.at[c, kind],
            device_id={"sta": me, "tpl": target},
            device_id_type=MESH,
        )

    pl.semaphore_wait(barrier, len(peers))
    for c in range(3):
        for kind in list(range(1, X)) + [0]:
            record_copy(c, kind).start()

    local[1].wait()
    for c in range(3):
        values = waves_ref[0, c].astype(F32)
        centred = values - jnp.mean(values, axis=-1, keepdims=True)
        spread = jnp.sqrt(jnp.mean(centred * centred, axis=-1, keepdims=True) + EPS)
        unit = centred / spread
        for a in range(WL):
            uw_ref[:, 3 * a + c, :] = unit[:, a * W : (a + 1) * W]

    for copy in local[2:]:
        copy.wait()

    owners = [lax.div(ps_ref[t, me], SL * N) for t in range(G)]
    keys = []
    for t in range(G):
        rank = jnp.int32(0)
        for before in range(t):
            rank = rank + (owners[before] == owners[t]).astype(jnp.int32)
        keys.append(owners[t] * CAP + rank)

    def packet_step(d, _):
        for j in range(CAP):
            chosen = jnp.int32(0)
            for t in range(G):
                chosen = jnp.where(keys[t] == d * CAP + j, t, chosen)
            row = pl.multiple_of((d * CAP + j) * 16, 16)
            pkt_ref[pl.ds(row, 16), :] = uw_ref[chosen].astype(BF16)
        return 0

    lax.fori_loop(0, S, packet_step, 0, unroll=4)

    def packet_copy(k):
        target = lax.rem(me + k, S)
        return pltpu.make_async_remote_copy(
            src_ref=pkt_ref.at[pl.ds(pl.multiple_of(target * CAP * 16, 16), CAP * 16)],
            dst_ref=pk_ref.at[pl.ds(pl.multiple_of(me * CAP * 16, 16), CAP * 16)],
            send_sem=p_send.at[k - 1],
            recv_sem=p_recv.at[k - 1],
            device_id={"sta": target, "tpl": g},
            device_id_type=MESH,
        )

    for k in range(1, S):
        packet_copy(k).start()
    own_packet = pl.ds(pl.multiple_of(me * CAP * 16, 16), CAP * 16)
    pk_ref[own_packet, :] = pkt_ref[own_packet, :]

    def table_step(p, _):
        count = jnp.int32(0)
        chosen = [jnp.int32(0)] * CAP
        for t in range(G):
            mine = (lax.div(ps_ref[t, p], SL * N) == me).astype(jnp.int32)
            place = mine * (count + 1)
            tp_tab[t * S + p] = jnp.where(
                place > 0, p * CAP + jnp.minimum(count, CAP - 1), NS
            )
            for j in range(CAP):
                chosen[j] = jnp.where(place == j + 1, t, chosen[j])
            count = count + mine
        for j in range(CAP):
            station = ps_ref[chosen[j], p] - me * SL * N
            station = jnp.minimum(jnp.maximum(station, 0), SL * N - 1)
            lag = pl_ref[chosen[j], p]
            holder = lax.div(station, SL)
            first = holder * RG + (station - holder * SL) * RPS
            row_tab[p * CAP + j] = first * H + lax.div(lag, STEP)
            b_tab[p * CAP + j] = lax.rem(lag, STEP)
            st_tab[p * CAP + j] = station
        return 0

    lax.fori_loop(0, S, table_step, 0)

    lane = lax.broadcasted_iota(jnp.int32, (8, W), 1)
    sub = lax.broadcasted_iota(jnp.int32, (8, W), 0)
    ones_k = lax.broadcasted_iota(jnp.int32, (W, 2 * W), 0)
    ones_r = lax.broadcasted_iota(jnp.int32, (W, 2 * W), 1)
    window = jnp.logical_and(ones_k >= ones_r, ones_r < W)
    window = jnp.logical_or(window, ones_k < ones_r - W).astype(F32).astype(BF16)
    window = jnp.concatenate([window] * 3, axis=0)

    def edge_sums(values):
        high = values.astype(BF16)
        rest = values - high.astype(F32)
        middle = rest.astype(BF16)
        low = (rest - middle.astype(F32)).astype(BF16)
        parts = jnp.concatenate([low, middle, high], axis=1)
        return jnp.dot(parts, window, preferred_element_type=F32)

    def shifted_rows(source, target, c, h):
        wide = lax.broadcasted_iota(jnp.int32, (RG, W), 1)
        now = source[pl.ds(0, RG), :]
        after = source[pl.ds(1, RG), :]
        row = h * (RG * H)
        target[c, pl.ds(row, RG, stride=H), :] = now
        for q in range(1, H):
            target[c, pl.ds(row + q, RG, stride=H), :] = jnp.where(
                wide < W - STEP * q,
                pltpu.roll(now, W - STEP * q, axis=1),
                pltpu.roll(after, W - STEP * q, axis=1),
            )

    def prepare(pair):
        RE = RG + 8
        held = [bufs[c][h] for h in pair for c in range(3)]
        for i, h in enumerate(pair):
            for c in range(3):
                shifted_rows(bufs[c].at[h], x4_ref, c, h)
        x = jnp.concatenate(held, axis=0)
        edges = edge_sums(jnp.concatenate([x, x * x], axis=0))
        d1_ref[...] = edges[:, :W]
        d2_ref[...] = edges[:, W:]
        tot_ref[...] = edges[:, :W] + edges[:, W:]
        for i, h in enumerate(pair):
            for c in range(3):
                means = []
                for q in range(2):
                    at = (q * 6 + i * 3 + c) * RE
                    total = d1_ref[pl.ds(at, RG), :] + d2_ref[pl.ds(at + WL, RG), :]
                    for a in range(1, WL):
                        total += tot_ref[pl.ds(at + a, RG), :]
                    means.append(total * (1.0 / L))
                one, two = means
                scale = lax.rsqrt(two - one * one + EPS) * (1.0 / L)
                sc_ref[i * 3 + c, pl.ds(0, RG), :] = scale
                shifted_rows(sc_ref.at[i * 3 + c], s4_ref, c, h)

    def toeplitz_step(slot, _):
        shift = b_tab[slot]
        unit = pk_ref[pl.ds(pl.multiple_of(slot * 16, 16), 16), :].astype(F32)
        unit = pltpu.roll(unit, shift, axis=1)
        zero_tile = jnp.zeros((8, W), F32)
        for c in range(3):
            rows = [
                jnp.broadcast_to(unit[3 * a + c : 3 * a + c + 1], (8, W)) for a in range(WL)
            ]
            strips = []
            for j in range(2):
                turned = [pltpu.roll(v, 8 * j, axis=1, stride=1, stride_axis=0) for v in rows]
                turned = [zero_tile] + turned + [zero_tile]
                keep = lane >= sub + (8 * j + shift)
                strips.append(
                    jnp.concatenate(
                        [jnp.where(keep, turned[a + 1], turned[a]) for a in range(KB)], axis=1
                    )
                )
            strip = jnp.concatenate(strips, axis=0).astype(BF16)
            toe_ref[slot, pl.ds(STEP * c, 16), :] = strip
            for j in range(16, STEP, 16):
                toe_ref[slot, pl.ds(STEP * c + j, 16), :] = pltpu.roll(strip, j, axis=1)
        return 0

    def slot_step(slot, _):
        row = row_tab[slot]
        shift = b_tab[slot]
        back = lax.rem(W - shift, W)
        frames = jnp.concatenate(
            [
                jnp.concatenate(
                    [x4_ref[c, pl.ds(row + H * a, MR), :] for a in range(KB)], axis=1
                )
                for c in range(3)
            ],
            axis=0,
        ).astype(BF16)
        corr = lax.dot_general(
            frames, toe_ref[slot], (((1,), (1,)), ((), ())), preferred_element_type=F32
        )
        terms = []
        for c in range(3):
            weight = mask_ref[c, st_tab[slot]].astype(F32)
            factor = pltpu.roll(s4_ref[c, pl.ds(row, MR), :], back, axis=1)
            mine = corr[MR * c : MR * (c + 1), STEP * c : STEP * (c + 1)]
            terms.append(mine * (factor[:, :STEP] * weight))
        acc_ref[slot] = terms[0] + terms[1] + terms[2]
        return 0

    def pass_on(c):
        for kind in range(1, X):
            record_copy(c, kind).wait_recv()
            record_copy(c, X - 1 + kind).start()

    for c in range(3):
        record_copy(c, 0).wait_recv()

    def two_strips(i, _):
        toeplitz_step(2 * i, 0)
        toeplitz_step(2 * i + 1, 0)
        return 0

    def pair_step(k, _):
        chip = lax.rem(xpos + X - k, X) * 2
        prepare((chip + core, chip + 1 - core))

        @pl.when(k == 0)
        def _():
            for c in range(3):
                pass_on(c)
            for other in range(1, S):
                packet_copy(other).wait_recv()

        lax.fori_loop(k * (NS // X // 2), (k + 1) * (NS // X // 2), two_strips, 0)

        @pl.when(k == 0)
        def _():
            for kind in range(X, 2 * X - 1):
                for c in range(3):
                    record_copy(c, kind).wait_recv()

        return 0

    lax.fori_loop(0, X, pair_step, 0)
    lax.fori_loop(0, NS, slot_step, 0, unroll=2)

    for group in range(NG):
        sums = []
        for t in range(group * TPG, (group + 1) * TPG):

            def add_pick(p, total):
                return total + acc_ref[tp_tab[t * S + p]]

            sums.append(lax.fori_loop(0, S, add_pick, jnp.zeros((MR, STEP), F32), unroll=8))
        side = jnp.concatenate(sums, axis=1)
        for d in range(S):
            part_ref[d, group // PK, pl.ds(group % PK * RD, RD), :] = side[RD * d : RD * (d + 1)]

    def sum_copy(k):
        target = lax.rem(me + k, S)
        return pltpu.make_async_remote_copy(
            src_ref=part_ref.at[target],
            dst_ref=land_ref.at[k - 1],
            send_sem=r_send.at[k - 1],
            recv_sem=r_recv.at[k - 1],
            device_id={"sta": target, "tpl": g},
            device_id_type=MESH,
        )

    for k in range(1, S):
        sum_copy(k).start()
    total = part_ref[me]
    for k in range(1, S):
        sum_copy(k).wait_recv()
        total = total + land_ref[k - 1]
    for t in range(G):
        m = t % TPG
        low = t // TPG % PK * RD
        for r in range(RD):
            out_ref[t : t + 1, STEP * r : STEP * (r + 1)] = total[
                t // TPG // PK, low + r : low + r + 1, STEP * m : STEP * (m + 1)
            ]

    for c in range(3):
        for kind in range(2 * X - 1):
            record_copy(c, kind).wait_send()
    for k in range(1, S):
        packet_copy(k).wait_send()
        sum_copy(k).wait_send()


def body(S, N, station_data, channel_mask, template_waves, pick_station, pick_lag):
    SL, samples = station_data.shape[1], station_data.shape[2]
    G, picks = pick_station.shape
    assert N % 2 == 0 and picks == S and template_waves.shape[1] == 1
    CAP = max(2, G // 8)
    RPS = samples // W
    RG = -(-(SL * RPS) // 8) * 8
    ND = NT // S
    STEP = 64 if ND % 64 == 0 else 16
    H = W // STEP
    MR = NT // STEP
    KB = -(-(L + 2 * STEP - 2) // W)
    PK = 8 // (ND // STEP)
    NP = -(-(G * STEP // W) // PK)
    X = N // 2
    NS = S * CAP
    dims = (S, N, SL, G, CAP, RPS, RG, ND, STEP)
    rows = N * RG * H
    vmem = pl.BlockSpec(memory_space=pltpu.VMEM)
    hbm = pl.BlockSpec(memory_space=pltpu.HBM)
    flops = 2 * NS * 3 * MR * STEP * KB * W
    result = pl.pallas_call(
        functools.partial(kernel, dims),
        out_shape=pltpu.VMEM((G, ND), F32),
        in_specs=[hbm] * 5,
        out_specs=vmem,
        scratch_shapes=[
            pltpu.VMEM(station_data.shape, F32),
            pltpu.VMEM((1, 3, G, L), BF16),
            pltpu.SMEM(channel_mask.shape, jnp.int32),
            pltpu.SMEM(pick_station.shape, jnp.int32),
            pltpu.SMEM(pick_lag.shape, jnp.int32),
            pltpu.VMEM((N, RG + 8, W), F32),
            pltpu.VMEM((N, RG + 8, W), F32),
            pltpu.VMEM((N, RG + 8, W), F32),
            pltpu.VMEM((12 * (RG + 8), W), F32),
            pltpu.VMEM((12 * (RG + 8), W), F32),
            pltpu.VMEM((12 * (RG + 8), W), F32),
            pltpu.VMEM((6, RG + 8, W), F32),
            pltpu.VMEM((3, rows, W), F32),
            pltpu.VMEM((3, rows, W), F32),
            pltpu.VMEM((G, 16, W), F32),
            pltpu.VMEM((NS * 16, W), BF16),
            pltpu.VMEM((NS * 16, W), BF16),
            pltpu.VMEM((NS, 3 * STEP, KB * W), BF16),
            pltpu.VMEM((NS + 1, MR, STEP), F32),
            pltpu.VMEM((S, NP, 8, W), F32),
            pltpu.VMEM((S - 1, NP, 8, W), F32),
            pltpu.SMEM((NS,), jnp.int32),
            pltpu.SMEM((NS,), jnp.int32),
            pltpu.SMEM((NS,), jnp.int32),
            pltpu.SMEM((G * S,), jnp.int32),
            pltpu.SemaphoreType.DMA((5,)),
            pltpu.SemaphoreType.DMA((3, 2 * X - 1)),
            pltpu.SemaphoreType.DMA((3, 2 * X - 1)),
            pltpu.SemaphoreType.DMA((S - 1,)),
            pltpu.SemaphoreType.DMA((S - 1,)),
            pltpu.SemaphoreType.DMA((S - 1,)),
            pltpu.SemaphoreType.DMA((S - 1,)),
        ],
        compiler_params=pltpu.CompilerParams(
            collective_id=0, has_side_effects=True, vmem_limit_bytes=63 * 1024 * 1024
        ),
        cost_estimate=pl.CostEstimate(flops=flops, bytes_accessed=1 << 20, transcendentals=0),
    )(station_data, jnp.transpose(template_waves, (1, 2, 0, 3)), channel_mask, pick_station, pick_lag)
    return result.T


def solution(mesh):
    in_specs = (
        P(None, ("sta", "tpl"), None),
        P(None, "sta"),
        P("tpl", "sta", None, None),
        P("tpl", None),
        P("tpl", None),
    )
    out_specs = P("sta", "tpl")
    run = functools.partial(body, mesh.shape["sta"], mesh.shape["tpl"])
    return jax.shard_map(run, mesh=mesh, in_specs=in_specs, out_specs=out_specs, check_vma=False)
```

```python
import functools

import jax
import jax.numpy as jnp
from jax import lax
from jax.experimental import pallas as pl
from jax.experimental.pallas import tpu as pltpu
from jax.sharding import PartitionSpec as P

NT = 1536
L = 640
LAGS = 1024
W = 128
EPS = 1e-05
MESH = pl.DeviceIdType.MESH
F32 = jnp.float32
BF16 = jnp.bfloat16

WL = L // W


def kernel(
    dims,
    data_hbm,
    waves_hbm,
    mask_hbm,
    ps_hbm,
    pl_hbm,
    out_ref,
    data_ref,
    waves_ref,
    mask_ref,
    ps_ref,
    pl_ref,
    buf0,
    buf1,
    buf2,
    d1_ref,
    d2_ref,
    tot_ref,
    sc_ref,
    x4_ref,
    s4_ref,
    uw_ref,
    pkt_ref,
    pk_ref,
    toe_ref,
    acc_ref,
    part_ref,
    land_ref,
    row_tab,
    b_tab,
    st_tab,
    tp_tab,
    l_sem,
    d_send,
    d_recv,
    p_send,
    p_recv,
    r_send,
    r_recv,
):
    S, N, SL, G, CAP, RPS, RG, ND, STEP = dims
    X = N // 2
    NS = S * CAP
    H = W // STEP
    MR = NT // STEP
    KB = -(-(L + 2 * STEP - 2) // W)
    TPG = W // STEP
    NG = G // TPG
    RD = ND // STEP
    PK = 8 // RD
    bufs = (buf0, buf1, buf2)
    me = lax.axis_index("sta")
    g = lax.axis_index("tpl")
    core = lax.rem(g, 2)
    xpos = g // 2
    mate = g + 1 - 2 * core
    peers = [{"sta": me, "tpl": mate}]
    far = []
    for k in range(1, X):
        far.append(lax.rem(xpos + k, X) * 2 + core)
        peers.append({"sta": me, "tpl": far[-1]})
    for k in range(1, S):
        peers.append({"sta": lax.rem(me + k, S), "tpl": g})

    local = [
        pltpu.make_async_copy(source, target, l_sem.at[i])
        for i, (source, target) in enumerate(
            [
                (data_hbm, data_ref),
                (waves_hbm, waves_ref),
                (ps_hbm, ps_ref),
                (pl_hbm, pl_ref),
                (mask_hbm, mask_ref),
            ]
        )
    ]
    for copy in local:
        copy.start()

    barrier = pltpu.get_barrier_semaphore()
    for peer in peers:
        pl.semaphore_signal(barrier, inc=1, device_id=peer, device_id_type=MESH)

    local[0].wait()
    for c in range(3):
        bufs[c][g, pl.ds(RG - 8, 8), :] = jnp.zeros((8, W), F32)
        for h in range(N):
            bufs[c][h, pl.ds(RG, 8), :] = jnp.zeros((8, W), F32)
        for m in range(2):
            sc_ref[m * 3 + c, pl.ds(RG, 8), :] = jnp.zeros((8, W), F32)
        for b in range(RPS):
            bufs[c][g, pl.ds(b, SL, stride=RPS), :] = data_ref[c, :, b * W : (b + 1) * W]
    acc_ref[NS] = jnp.zeros((MR, STEP), F32)

    def record_copy(c, kind):
        if kind == 0:
            source, target = g, mate
        elif kind < X:
            source, target = g, far[kind - 1]
        else:
            source, target = lax.rem(xpos + X - (kind - X + 1), X) * 2 + core, mate
        return pltpu.make_async_remote_copy(
            src_ref=bufs[c].at[source, pl.ds(0, RG)],
            dst_ref=bufs[c].at[source, pl.ds(0, RG)],
            send_sem=d_send.at[c, kind],
            recv_sem=d_recv.at[c, kind],
            device_id={"sta": me, "tpl": target},
            device_id_type=MESH,
        )

    pl.semaphore_wait(barrier, len(peers))
    for c in range(3):
        for kind in list(range(1, X)) + [0]:
            record_copy(c, kind).start()

    local[1].wait()
    for c in range(3):
        values = waves_ref[0, c].astype(F32)
        centred = values - jnp.mean(values, axis=-1, keepdims=True)
        spread = jnp.sqrt(jnp.mean(centred * centred, axis=-1, keepdims=True) + EPS)
        unit = centred / spread
        for a in range(WL):
            uw_ref[:, 3 * a + c, :] = unit[:, a * W : (a + 1) * W]

    for copy in local[2:]:
        copy.wait()

    owners = [lax.div(ps_ref[t, me], SL * N) for t in range(G)]
    keys = []
    for t in range(G):
        rank = jnp.int32(0)
        for before in range(t):
            rank = rank + (owners[before] == owners[t]).astype(jnp.int32)
        keys.append(owners[t] * CAP + rank)

    def packet_step(d, _):
        for j in range(CAP):
            chosen = jnp.int32(0)
            for t in range(G):
                chosen = jnp.where(keys[t] == d * CAP + j, t, chosen)
            row = pl.multiple_of((d * CAP + j) * 16, 16)
            pkt_ref[pl.ds(row, 16), :] = uw_ref[chosen].astype(BF16)
        return 0

    lax.fori_loop(0, S, packet_step, 0, unroll=4)

    def packet_copy(k):
        target = lax.rem(me + k, S)
        return pltpu.make_async_remote_copy(
            src_ref=pkt_ref.at[pl.ds(pl.multiple_of(target * CAP * 16, 16), CAP * 16)],
            dst_ref=pk_ref.at[pl.ds(pl.multiple_of(me * CAP * 16, 16), CAP * 16)],
            send_sem=p_send.at[k - 1],
            recv_sem=p_recv.at[k - 1],
            device_id={"sta": target, "tpl": g},
            device_id_type=MESH,
        )

    for k in range(1, S):
        packet_copy(k).start()
    own_packet = pl.ds(pl.multiple_of(me * CAP * 16, 16), CAP * 16)
    pk_ref[own_packet, :] = pkt_ref[own_packet, :]

    def table_step(p, _):
        count = jnp.int32(0)
        chosen = [jnp.int32(0)] * CAP
        for t in range(G):
            mine = (lax.div(ps_ref[t, p], SL * N) == me).astype(jnp.int32)
            place = mine * (count + 1)
            tp_tab[t * S + p] = jnp.where(
                place > 0, p * CAP + jnp.minimum(count, CAP - 1), NS
            )
            for j in range(CAP):
                chosen[j] = jnp.where(place == j + 1, t, chosen[j])
            count = count + mine
        for j in range(CAP):
            station = ps_ref[chosen[j], p] - me * SL * N
            station = jnp.minimum(jnp.maximum(station, 0), SL * N - 1)
            lag = pl_ref[chosen[j], p]
            holder = lax.div(station, SL)
            first = holder * RG + (station - holder * SL) * RPS
            row_tab[p * CAP + j] = first * H + lax.div(lag, STEP)
            b_tab[p * CAP + j] = lax.rem(lag, STEP)
            st_tab[p * CAP + j] = station
        return 0

    lax.fori_loop(0, S, table_step, 0)

    lane = lax.broadcasted_iota(jnp.int32, (8, W), 1)
    sub = lax.broadcasted_iota(jnp.int32, (8, W), 0)
    ones_k = lax.broadcasted_iota(jnp.int32, (W, 2 * W), 0)
    ones_r = lax.broadcasted_iota(jnp.int32, (W, 2 * W), 1)
    window = jnp.logical_and(ones_k >= ones_r, ones_r < W)
    window = jnp.logical_or(window, ones_k < ones_r - W).astype(F32).astype(BF16)
    window = jnp.concatenate([window] * 3, axis=0)

    def edge_sums(values):
        high = values.astype(BF16)
        rest = values - high.astype(F32)
        middle = rest.astype(BF16)
        low = (rest - middle.astype(F32)).astype(BF16)
        parts = jnp.concatenate([low, middle, high], axis=1)
        return jnp.dot(parts, window, preferred_element_type=F32)

    def shifted_rows(source, target, c, h):
        wide = lax.broadcasted_iota(jnp.int32, (RG, W), 1)
        now = source[pl.ds(0, RG), :]
        after = source[pl.ds(1, RG), :]
        row = h * (RG * H)
        target[c, pl.ds(row, RG, stride=H), :] = now
        for q in range(1, H):
            target[c, pl.ds(row + q, RG, stride=H), :] = jnp.where(
                wide < W - STEP * q,
                pltpu.roll(now, W - STEP * q, axis=1),
                pltpu.roll(after, W - STEP * q, axis=1),
            )

    def prepare(pair):
        RE = RG + 8
        held = [bufs[c][h] for h in pair for c in range(3)]
        for i, h in enumerate(pair):
            for c in range(3):
                shifted_rows(bufs[c].at[h], x4_ref, c, h)
        x = jnp.concatenate(held, axis=0)
        edges = edge_sums(jnp.concatenate([x, x * x], axis=0))
        d1_ref[...] = edges[:, :W]
        d2_ref[...] = edges[:, W:]
        tot_ref[...] = edges[:, :W] + edges[:, W:]
        for i, h in enumerate(pair):
            for c in range(3):
                means = []
                for q in range(2):
                    at = (q * 6 + i * 3 + c) * RE
                    total = d1_ref[pl.ds(at, RG), :] + d2_ref[pl.ds(at + WL, RG), :]
                    for a in range(1, WL):
                        total += tot_ref[pl.ds(at + a, RG), :]
                    means.append(total * (1.0 / L))
                one, two = means
                scale = lax.rsqrt(two - one * one + EPS) * (1.0 / L)
                sc_ref[i * 3 + c, pl.ds(0, RG), :] = scale
                shifted_rows(sc_ref.at[i * 3 + c], s4_ref, c, h)

    def toeplitz_step(slot, _):
        shift = b_tab[slot]
        unit = pk_ref[pl.ds(pl.multiple_of(slot * 16, 16), 16), :].astype(F32)
        unit = pltpu.roll(unit, shift, axis=1)
        zero_tile = jnp.zeros((8, W), F32)
        for c in range(3):
            rows = [
                jnp.broadcast_to(unit[3 * a + c : 3 * a + c + 1], (8, W)) for a in range(WL)
            ]
            strips = []
            for j in range(2):
                turned = [pltpu.roll(v, 8 * j, axis=1, stride=1, stride_axis=0) for v in rows]
                turned = [zero_tile] + turned + [zero_tile]
                keep = lane >= sub + (8 * j + shift)
                strips.append(
                    jnp.concatenate(
                        [jnp.where(keep, turned[a + 1], turned[a]) for a in range(KB)], axis=1
                    )
                )
            strip = jnp.concatenate(strips, axis=0).astype(BF16)
            toe_ref[slot, pl.ds(STEP * c, 16), :] = strip
            for j in range(16, STEP, 16):
                toe_ref[slot, pl.ds(STEP * c + j, 16), :] = pltpu.roll(strip, j, axis=1)
        return 0

    def slot_step(slot, _):
        row = row_tab[slot]
        shift = b_tab[slot]
        back = lax.rem(W - shift, W)
        frames = jnp.concatenate(
            [
                jnp.concatenate(
                    [x4_ref[c, pl.ds(row + H * a, MR), :] for a in range(KB)], axis=1
                )
                for c in range(3)
            ],
            axis=0,
        ).astype(BF16)
        corr = lax.dot_general(
            frames, toe_ref[slot], (((1,), (1,)), ((), ())), preferred_element_type=F32
        )
        terms = []
        for c in range(3):
            weight = mask_ref[c, st_tab[slot]].astype(F32)
            factor = pltpu.roll(s4_ref[c, pl.ds(row, MR), :], back, axis=1)
            mine = corr[MR * c : MR * (c + 1), STEP * c : STEP * (c + 1)]
            terms.append(mine * (factor[:, :STEP] * weight))
        acc_ref[slot] = terms[0] + terms[1] + terms[2]
        return 0

    def pass_on(c):
        for kind in range(1, X):
            record_copy(c, kind).wait_recv()
            record_copy(c, X - 1 + kind).start()

    for c in range(3):
        record_copy(c, 0).wait_recv()

    def two_strips(i, _):
        toeplitz_step(2 * i, 0)
        toeplitz_step(2 * i + 1, 0)
        return 0

    def pair_step(k, _):
        chip = lax.rem(xpos + X - k, X) * 2
        prepare((chip + core, chip + 1 - core))

        @pl.when(k == 0)
        def _():
            for other in range(1, S):
                packet_copy(other).wait_recv()

            def half_step(half, _):
                lax.fori_loop(half * (NS // 4), (half + 1) * (NS // 4), two_strips, 0)

                @pl.when(half == 0)
                def _():
                    for c in range(3):
                        pass_on(c)

                return 0

            lax.fori_loop(0, 2, half_step, 0)
            for kind in range(X, 2 * X - 1):
                for c in range(3):
                    record_copy(c, kind).wait_recv()

        return 0

    lax.fori_loop(0, X, pair_step, 0)
    lax.fori_loop(0, NS, slot_step, 0, unroll=2)

    for group in range(NG):
        sums = []
        for t in range(group * TPG, (group + 1) * TPG):

            def add_pick(p, total):
                return total + acc_ref[tp_tab[t * S + p]]

            sums.append(lax.fori_loop(0, S, add_pick, jnp.zeros((MR, STEP), F32), unroll=8))
        side = jnp.concatenate(sums, axis=1)
        for d in range(S):
            part_ref[d, group // PK, pl.ds(group % PK * RD, RD), :] = side[RD * d : RD * (d + 1)]

    def sum_copy(k):
        target = lax.rem(me + k, S)
        return pltpu.make_async_remote_copy(
            src_ref=part_ref.at[target],
            dst_ref=land_ref.at[k - 1],
            send_sem=r_send.at[k - 1],
            recv_sem=r_recv.at[k - 1],
            device_id={"sta": target, "tpl": g},
            device_id_type=MESH,
        )

    for k in range(1, S):
        sum_copy(k).start()
    total = part_ref[me]
    for k in range(1, S):
        sum_copy(k).wait_recv()
        total = total + land_ref[k - 1]
    for t in range(G):
        m = t % TPG
        low = t // TPG % PK * RD
        for r in range(RD):
            out_ref[t : t + 1, STEP * r : STEP * (r + 1)] = total[
                t // TPG // PK, low + r : low + r + 1, STEP * m : STEP * (m + 1)
            ]

    for c in range(3):
        for kind in range(2 * X - 1):
            record_copy(c, kind).wait_send()
    for k in range(1, S):
        packet_copy(k).wait_send()
        sum_copy(k).wait_send()


def body(S, N, station_data, channel_mask, template_waves, pick_station, pick_lag):
    SL, samples = station_data.shape[1], station_data.shape[2]
    G, picks = pick_station.shape
    assert N % 2 == 0 and picks == S and template_waves.shape[1] == 1
    CAP = max(2, G // 8)
    RPS = samples // W
    RG = -(-(SL * RPS) // 8) * 8
    ND = NT // S
    STEP = 64 if ND % 64 == 0 else 16
    H = W // STEP
    MR = NT // STEP
    KB = -(-(L + 2 * STEP - 2) // W)
    PK = 8 // (ND // STEP)
    NP = -(-(G * STEP // W) // PK)
    X = N // 2
    NS = S * CAP
    dims = (S, N, SL, G, CAP, RPS, RG, ND, STEP)
    rows = N * RG * H
    vmem = pl.BlockSpec(memory_space=pltpu.VMEM)
    hbm = pl.BlockSpec(memory_space=pltpu.HBM)
    flops = 2 * NS * 3 * MR * STEP * KB * W
    result = pl.pallas_call(
        functools.partial(kernel, dims),
        out_shape=pltpu.VMEM((G, ND), F32),
        in_specs=[hbm] * 5,
        out_specs=vmem,
        scratch_shapes=[
            pltpu.VMEM(station_data.shape, F32),
            pltpu.VMEM((1, 3, G, L), BF16),
            pltpu.SMEM(channel_mask.shape, jnp.int32),
            pltpu.SMEM(pick_station.shape, jnp.int32),
            pltpu.SMEM(pick_lag.shape, jnp.int32),
            pltpu.VMEM((N, RG + 8, W), F32),
            pltpu.VMEM((N, RG + 8, W), F32),
            pltpu.VMEM((N, RG + 8, W), F32),
            pltpu.VMEM((12 * (RG + 8), W), F32),
            pltpu.VMEM((12 * (RG + 8), W), F32),
            pltpu.VMEM((12 * (RG + 8), W), F32),
            pltpu.VMEM((6, RG + 8, W), F32),
            pltpu.VMEM((3, rows, W), F32),
            pltpu.VMEM((3, rows, W), F32),
            pltpu.VMEM((G, 16, W), F32),
            pltpu.VMEM((NS * 16, W), BF16),
            pltpu.VMEM((NS * 16, W), BF16),
            pltpu.VMEM((NS, 3 * STEP, KB * W), BF16),
            pltpu.VMEM((NS + 1, MR, STEP), F32),
            pltpu.VMEM((S, NP, 8, W), F32),
            pltpu.VMEM((S - 1, NP, 8, W), F32),
            pltpu.SMEM((NS,), jnp.int32),
            pltpu.SMEM((NS,), jnp.int32),
            pltpu.SMEM((NS,), jnp.int32),
            pltpu.SMEM((G * S,), jnp.int32),
            pltpu.SemaphoreType.DMA((5,)),
            pltpu.SemaphoreType.DMA((3, 2 * X - 1)),
            pltpu.SemaphoreType.DMA((3, 2 * X - 1)),
            pltpu.SemaphoreType.DMA((S - 1,)),
            pltpu.SemaphoreType.DMA((S - 1,)),
            pltpu.SemaphoreType.DMA((S - 1,)),
            pltpu.SemaphoreType.DMA((S - 1,)),
        ],
        compiler_params=pltpu.CompilerParams(
            collective_id=0, has_side_effects=True, vmem_limit_bytes=63 * 1024 * 1024
        ),
        cost_estimate=pl.CostEstimate(flops=flops, bytes_accessed=1 << 20, transcendentals=0),
    )(station_data, jnp.transpose(template_waves, (1, 2, 0, 3)), channel_mask, pick_station, pick_lag)
    return result.T


def solution(mesh):
    in_specs = (
        P(None, ("sta", "tpl"), None),
        P(None, "sta"),
        P("tpl", "sta", None, None),
        P("tpl", None),
        P("tpl", None),
    )
    out_specs = P("sta", "tpl")
    run = functools.partial(body, mesh.shape["sta"], mesh.shape["tpl"])
    return jax.shard_map(run, mesh=mesh, in_specs=in_specs, out_specs=out_specs, check_vma=False)
```
